256 devices in a mesh: stretch: 32 (over z, x), tile: 8 (over y, core).
Axes of the slice: x: 4, y: 4, z: 8, core: 2. Of those that a mesh axis runs over, the one named last changes fastest.
Arguments:
- video: bfloat16 [544, 16, 320, 128], P('stretch', 'tile'), may hold values from -6 to 6
- clip_table: int32 [2, 16], replicated, may hold values from 1 to 17, as said below
- w_spatial: bfloat16 [3, 3, 128, 128], replicated, may hold values from -0.1875 to 0.1875
- w_temporal: bfloat16 [3, 128, 128], replicated, may hold values from -0.3125 to 0.3125
- w_down: bfloat16 [512, 256], replicated, may hold values from -0.25 to 0.25
- w_query: bfloat16 [256, 256], replicated
- w_key: bfloat16 [256, 256], replicated
- w_value: bfloat16 [256, 256], replicated, may hold values from -0.375 to 0.375
- w_out: bfloat16 [256, 256], replicated, may hold values from -0.375 to 0.375
Outputs:
- encoded: bfloat16 [544, 8, 160, 256], P('stretch', 'tile')
The draws below stay inside these ranges and needn't reach their ends.
Inputs may be any that keep to these rules, and one draw needn't show every extreme that they name: `clip_table`: row 0: clips are laid end to end over the 32 stretches in order, each of 1 to 3 stretches, summing to 32, some clip exactly 3. Row 1: 1 to 17 real frames, some clip exactly 17.
All inputs are finite; a program needn't handle non-finite values.
Results may differ from the reference program's by a relative error of at most 0.015.
Values may be sent and summed in bfloat16 or wider, within the bound.
No kernel may reach another device: no remote copies, remote signals or barrier semaphores. Data moves between devices by JAX's collectives and lax.ppermute only.
A program may use at most 128 MiB of HBM per device.

```python
import math
import jax
import jax.numpy as jnp
from jax import lax

C1 = 128
C2 = 256
WIDTH = 320
STRETCH_FR = 17
CLIP_MOST = 3
CLIPS = 16
FRAMES = 544
HEIGHT = 16
HALF_H = 8
HALF_W = 160
N_STRETCH = 32


def draw_w_query(key, part):
    key = jax.random.fold_in(key, 1)
    return (jax.random.normal(key, (C2, C2), jnp.float32) / C2 ** 0.5).astype(jnp.bfloat16)


def draw_w_key(key, part):
    key = jax.random.fold_in(key, 2)
    return (jax.random.normal(key, (C2, C2), jnp.float32) / C2 ** 0.5).astype(jnp.bfloat16)


def draw_clip_table(key, part):
    key = jax.random.fold_in(key, 5)
    pick_key, order_key, frame_key, full_key = jax.random.split(key, 4)
    stretch_total = FRAMES // STRETCH_FR
    spare = CLIP_MOST - 1
    extra = stretch_total - CLIPS - spare
    slot_count = CLIPS * spare
    chosen = jax.random.randint(pick_key, (), 0, CLIPS)
    slot_owner = jnp.arange(slot_count, dtype=jnp.int32) // spare
    priority = jax.random.permutation(order_key, slot_count).astype(jnp.int32)
    ranked = jnp.where(slot_owner != chosen, priority, priority + slot_count)
    ordering = jnp.argsort(ranked, stable=True)
    taken = jnp.zeros((slot_count,), jnp.int32).at[ordering[:extra]].set(1)
    clip_ids = jnp.arange(CLIPS, dtype=jnp.int32)
    owned = (slot_owner[None, :] == clip_ids[:, None]).astype(jnp.int32)
    counts = 1 + jnp.sum(owned * taken[None, :], axis=1) + spare * (clip_ids == chosen).astype(jnp.int32)
    last = jax.random.randint(frame_key, (CLIPS,), 1, STRETCH_FR + 1)
    full = jax.random.randint(full_key, (), 0, CLIPS)
    last = jnp.where(clip_ids == full, STRETCH_FR, last)
    return jnp.stack([counts, last]).astype(jnp.int32)


def level_of(own_key, extent, pieces, low, largest):
    def one(position, parts):
        draws = jax.random.uniform(jax.random.fold_in(jax.random.fold_in(own_key, 6), position), (parts,), jnp.float32, low / len(pieces), largest / len(pieces))
        return jnp.repeat(jnp.exp(draws), extent[position] // parts).reshape((-1,) + (1,) * (len(extent) - position - 1))

    factor_of = one(*pieces[0])
    for cut in pieces[1:]:
        factor_of = factor_of * one(*cut)
    return factor_of


def gaussian(stream_key, shape, width, reach, shards=(), kind=jnp.bfloat16):
    level = level_of(stream_key, shape, shards, -0.22, 0.18) if shards else 1.0
    entries = jax.random.normal(stream_key, shape, jnp.float32) * width * level
    return jnp.minimum(jnp.maximum(entries, -reach), reach).astype(kind)


def setup_inputs(seed: int = 0) -> dict:
    seeds = jax.random.split(jax.random.key(seed), 10)
    video = gaussian(seeds[0], (FRAMES, HEIGHT, WIDTH, C1), 1.0, 6.0, ((0, 32), (1, 8)))
    clip_table = draw_clip_table(jax.random.fold_in(seeds[9], 71), 0)
    w_spatial = gaussian(seeds[2], (3, 3, C1, C1), (9 * C1) ** -0.5, 0.1875)
    w_temporal = gaussian(seeds[3], (3, C1, C1), (3 * C1) ** -0.5, 0.3125)
    w_down = gaussian(seeds[4], (4 * C1, C2), (4 * C1) ** -0.5, 0.25)
    w_query = draw_w_query(jax.random.fold_in(seeds[9], 71), 0)
    w_key = draw_w_key(jax.random.fold_in(seeds[9], 71), 0)
    w_value = gaussian(seeds[7], (C2, C2), C2 ** -0.5, 0.375)
    w_out = gaussian(seeds[8], (C2, C2), C2 ** -0.5, 0.375)
    return {"video": video, "clip_table": clip_table, "w_spatial": w_spatial, "w_temporal": w_temporal, "w_down": w_down, "w_query": w_query, "w_key": w_key, "w_value": w_value, "w_out": w_out}


def conv_plane(planes, weights, row_pad):
    return lax.conv_general_dilated(planes, weights, (1, 1), ((row_pad, row_pad), (1, 1)), dimension_numbers=('NHWC', 'HWIO', 'NHWC'), preferred_element_type=jnp.float32)

def wavelet(planes):
    frames, row_count, columns, channels = planes.shape
    grid = planes.astype(jnp.float32).reshape(frames, row_count // 2, 2, columns // 2, 2, channels)
    upper_left = grid[:, :, 0, :, 0]
    upper_right = grid[:, :, 0, :, 1]
    lower_left = grid[:, :, 1, :, 0]
    lower_right = grid[:, :, 1, :, 1]
    joined = jnp.concatenate([upper_left + upper_right + lower_left + lower_right, upper_left - upper_right + lower_left - lower_right, upper_left + upper_right - lower_left - lower_right, upper_left - upper_right - lower_left + lower_right], axis=-1)
    return (joined * 0.5).astype(jnp.bfloat16)

def normalize(latent):
    values = latent.astype(jnp.float32)
    return (values * lax.rsqrt(lax.optimization_barrier(jnp.mean(values * values, axis=-1, keepdims=True)) + 1e-06)).astype(jnp.bfloat16)

def project(normed, weights):
    lead_shape = normed.shape[:-1]
    flat = jnp.dot(normed.reshape(-1, normed.shape[-1]), weights, preferred_element_type=jnp.float32)
    return flat.astype(jnp.bfloat16).reshape(lead_shape + (weights.shape[1],))

def reference(video, clip_table, w_spatial, w_temporal, w_down, w_query, w_key, w_value, w_out):
    clip_stretches = clip_table[0]
    last_frames = clip_table[1]
    clip_ends = jnp.cumsum(clip_stretches).astype(jnp.int32)
    clip_starts = clip_ends - clip_stretches

    def front(stretch_index):
        current = lax.dynamic_slice_in_dim(video, stretch_index * STRETCH_FR, STRETCH_FR, 0)
        earlier = lax.dynamic_slice_in_dim(video, jnp.maximum(stretch_index * STRETCH_FR - 2, 0).astype(jnp.int32), 2, 0)
        plane_out = conv_plane(current, w_spatial, 1).astype(jnp.bfloat16)
        tail_slab = conv_plane(earlier, w_spatial, 1).astype(jnp.bfloat16)
        is_first = jnp.any(clip_starts == stretch_index)
        cache_slab = jnp.where(is_first, jnp.broadcast_to(plane_out[:1], tail_slab.shape), tail_slab)
        extended = jnp.concatenate([cache_slab, plane_out], axis=0)
        temporal_out = jnp.zeros(current.shape, jnp.float32)
        for tap_index in range(3):
            temporal_out = temporal_out + jnp.einsum('fhwc,cd->fhwd', extended[tap_index:tap_index + STRETCH_FR].astype(jnp.float32), w_temporal[tap_index].astype(jnp.float32))
        residual_sum = (current.astype(jnp.float32) + jax.nn.silu(temporal_out)).astype(jnp.bfloat16)
        subbands = wavelet(residual_sum)
        latent = jnp.dot(subbands.reshape(-1, 4 * C1), w_down, preferred_element_type=jnp.float32)
        return latent.astype(jnp.bfloat16).reshape(STRETCH_FR, HALF_H * HALF_W, C2)
    stretch_ids = jnp.arange(N_STRETCH, dtype=jnp.int32)
    latent_all = lax.map(front, stretch_ids).reshape(FRAMES, HALF_H * HALF_W, C2)
    clip_of_stretch = lax.optimization_barrier(jnp.sum((clip_ends[None, :] <= stretch_ids[:, None]).astype(jnp.int32), axis=1))
    window_len = CLIP_MOST * STRETCH_FR
    score_scale = 1.0 / math.sqrt(C2)

    def attend(stretch_index):
        window_start = (jnp.maximum(stretch_index - (CLIP_MOST - 1), 0) * STRETCH_FR).astype(jnp.int32)
        window = lax.dynamic_slice_in_dim(latent_all, window_start, window_len, 0)
        current = lax.dynamic_slice_in_dim(latent_all, (stretch_index * STRETCH_FR).astype(jnp.int32), STRETCH_FR, 0)
        queries = project(normalize(current), w_query)
        window_normed = normalize(window)
        key_rows = project(window_normed, w_key)
        values = project(window_normed, w_value)
        key_frames = window_start + jnp.arange(window_len, dtype=jnp.int32)
        query_frames = stretch_index * STRETCH_FR + jnp.arange(STRETCH_FR, dtype=jnp.int32)
        key_clip = jnp.take(clip_of_stretch, key_frames // STRETCH_FR)
        allowed = (key_clip[None, :] == clip_of_stretch[stretch_index]) & (key_frames[None, :] <= query_frames[:, None])
        scores = jnp.einsum('tpc,spc->pts', queries.astype(jnp.float32), key_rows.astype(jnp.float32)) * score_scale
        masked = jnp.where(allowed[None], scores, -1e+30)
        row_max = lax.optimization_barrier(jnp.max(masked, axis=-1, keepdims=True))
        exp_scores = jnp.exp(masked - row_max)
        probs = (exp_scores / lax.optimization_barrier(jnp.sum(exp_scores, axis=-1, keepdims=True))).astype(jnp.bfloat16)
        attended = jnp.einsum('pts,spc->tpc', probs.astype(jnp.float32), values.astype(jnp.float32)).astype(jnp.bfloat16)
        update = jnp.dot(attended.reshape(-1, C2), w_out, preferred_element_type=jnp.float32)
        result = current.astype(jnp.float32) + update.reshape(STRETCH_FR, HALF_H * HALF_W, C2)
        is_last = clip_ends - 1 == stretch_index
        valid_count = jnp.where(jnp.any(is_last), jnp.sum(jnp.where(is_last, last_frames, 0)), STRETCH_FR)
        frame_keep = jnp.arange(STRETCH_FR, dtype=jnp.int32) < valid_count
        result = jnp.where(frame_keep[:, None, None], result, 0.0)
        return result.astype(jnp.bfloat16).reshape(STRETCH_FR, HALF_H, HALF_W, C2)
    return lax.map(attend, stretch_ids).reshape(FRAMES, HALF_H, HALF_W, C2)
```

```python
import functools

import jax
import jax.numpy as jnp
from jax import lax
from jax.experimental import pallas as pl
from jax.experimental.pallas import tpu as pltpu
from jax.sharding import PartitionSpec as P

F32 = jnp.float32
BF16 = jnp.bfloat16
FRAMES = 17
COLS = 320
HALF = 160
C1 = 128
C2 = 256
GROUP = 16
BIG = 3.0e38


def shift_perm(axis, by):
    count = lax.axis_size(axis)
    return [(i, i + by) for i in range(count) if 0 <= i + by < count]


def send(x, axis, by):
    return lax.ppermute(x, axis, shift_perm(axis, by))


def conv_frames(count, at, vid, up, down, w_conv, planes):
    row = lax.broadcasted_iota(jnp.int32, (COLS, 2 * C1), 0)

    def conv(f, _):
        x = jnp.concatenate([up[f], vid[f, 0], vid[f, 1], down[f]], axis=1)
        y = jnp.dot(x, w_conv[...], preferred_element_type=F32)
        left = pltpu.roll(y[:, : 2 * C1], 1, 0)
        right = pltpu.roll(y[:, 4 * C1 :], COLS - 1, 0)
        plane = (
            y[:, 2 * C1 : 4 * C1]
            + jnp.where(row == 0, 0.0, left)
            + jnp.where(row == COLS - 1, 0.0, right)
        )
        planes[f + at] = plane.astype(BF16)
        return 0

    lax.fori_loop(0, count, conv, 0)


def latent_frames(count, at, vid, planes, mixed, w_time, w_down, latent):
    def rest(g, _):
        f = g + at
        x = jnp.concatenate([planes[g], planes[g + 1], planes[g + 2]], axis=1)
        v = jnp.dot(x, w_time[...], preferred_element_type=F32)
        gate = v * (0.5 * jnp.tanh(0.5 * v) + 0.5)
        residual = jnp.concatenate([vid[f, 0], vid[f, 1]], axis=1).astype(F32)
        m = residual + gate
        mixed[0:COLS, :] = m[:, :C1]
        mixed[COLS:, :] = m[:, C1:]
        p = mixed[pl.ds(0, HALF, stride=2), :]
        q = mixed[pl.ds(1, HALF, stride=2), :]
        r = mixed[pl.ds(COLS, HALF, stride=2), :]
        s = mixed[pl.ds(COLS + 1, HALF, stride=2), :]
        top, low = p + q, r + s
        top_d, low_d = p - q, r - s
        bands = jnp.concatenate([top + low, top_d + low_d, top - low, top_d - low_d], axis=1)
        out = jnp.dot((bands * 0.5).astype(BF16), w_down[...], preferred_element_type=F32)
        latent[g] = out.astype(BF16)
        return 0

    lax.fori_loop(0, count, rest, 0)


def front_a_kernel(first, count, video, up, down, w_conv, w_time, w_down,
                   latent, planes_out, vid, planes, mixed, sems):
    copy = pltpu.make_async_copy(video.at[pl.ds(first, count)], vid, sems.at[0])
    copy.start()
    copy.wait()
    conv_frames(count, 0, vid, up, down, w_conv, planes)
    latent_frames(count - 2, 2, vid, planes, mixed, w_time, w_down, latent)
    planes_out[0:2] = planes[0:2]
    planes_out[2:4] = planes[count - 2 : count]


def front_a(video, up, down, w_conv, w_time, w_down, first):
    count = FRAMES - first
    vm = pl.BlockSpec(memory_space=pltpu.VMEM)
    return pl.pallas_call(
        functools.partial(front_a_kernel, first, count),
        out_shape=(
            jax.ShapeDtypeStruct((count - 2, HALF, C2), BF16),
            jax.ShapeDtypeStruct((4, COLS, 2 * C1), BF16),
        ),
        in_specs=[pl.BlockSpec(memory_space=pl.ANY)] + [vm] * 5,
        out_specs=(vm, vm),
        scratch_shapes=[
            pltpu.VMEM((count, 2, COLS, C1), BF16),
            pltpu.VMEM((count, COLS, 2 * C1), BF16),
            pltpu.VMEM((2 * COLS, C1), F32),
            pltpu.SemaphoreType.DMA((1,)),
        ],
        compiler_params=pltpu.CompilerParams(vmem_limit_bytes=48 * 2**20),
        name="front_a",
    )(video, up, down, w_conv, w_time, w_down)


def front_b_kernel(count, offset, video, up, down, tail, after, w_conv, w_time, w_down,
                   latent, vid, planes, mixed, sems):
    copy = pltpu.make_async_copy(video.at[pl.ds(0, count + 2)], vid, sems.at[0])
    copy.start()
    planes[count + 2 : count + 4] = after[0:2]
    copy.wait()
    conv_frames(count, 2, vid, up, down, w_conv, planes)
    is_start = offset[0] == 0

    @pl.when(is_start)
    def _():
        planes[0] = planes[2]
        planes[1] = planes[2]

    @pl.when(jnp.logical_not(is_start))
    def _():
        planes[0:2] = tail[...]

    latent_frames(count + 2, 0, vid, planes, mixed, w_time, w_down, latent)


def front_b(video, up, down, tail, after, offset, w_conv, w_time, w_down, count):
    vm = pl.BlockSpec(memory_space=pltpu.VMEM)
    return pl.pallas_call(
        functools.partial(front_b_kernel, count),
        out_shape=jax.ShapeDtypeStruct((count + 2, HALF, C2), BF16),
        in_specs=[pl.BlockSpec(memory_space=pltpu.SMEM), pl.BlockSpec(memory_space=pl.ANY)] + [vm] * 7,
        out_specs=vm,
        scratch_shapes=[
            pltpu.VMEM((count + 2, 2, COLS, C1), BF16),
            pltpu.VMEM((count + 4, COLS, 2 * C1), BF16),
            pltpu.VMEM((2 * COLS, C1), F32),
            pltpu.SemaphoreType.DMA((1,)),
        ],
        compiler_params=pltpu.CompilerParams(vmem_limit_bytes=48 * 2**20),
        name="front_b",
    )(offset, video, up, down, tail, after, w_conv, w_time, w_down)


KEYS = 3 * FRAMES * 8
KEYS_PAD = 512
ROWS = FRAMES * 8


def attend_kernel(split, info, lat_b, lat_a, one_b, one_a, two_b, two_a, w_q, w_kv, w_o, out, bound):
    offset = info[0]
    valid = info[1]
    r = lax.broadcasted_iota(jnp.int32, (ROWS, KEYS_PAD), 0)
    c = lax.broadcasted_iota(jnp.int32, (ROWS, KEYS_PAD), 1)
    same = jnp.bitwise_and(r, 7) == jnp.bitwise_and(c, 7)
    t = jnp.right_shift(r, 3)
    s = jnp.right_shift(c, 3)
    low = jnp.where(offset >= 2, 0, jnp.where(offset == 1, FRAMES, 2 * FRAMES))
    allowed = same & (s >= low) & (s <= t + 2 * FRAMES)
    bound[...] = jnp.where(allowed, BIG, -1e30)

    def normed(x):
        return (x * lax.rsqrt(jnp.mean(x * x, axis=-1, keepdims=True) + 1e-6)).astype(BF16)

    def halves(x, frames):
        x = x.reshape(frames, 2, 8, C2)
        return [x[:, h].reshape(frames * 8, C2).astype(BF16) for h in range(2)]

    def block(g, _):
        at = pl.ds(pl.multiple_of(g * GROUP, GROUP), GROUP)
        parts = [two_b, two_a, one_b, one_a, lat_b, lat_a]
        x = jnp.concatenate([p[:, at, :] for p in parts], axis=0)
        x = x.reshape(3 * FRAMES * GROUP, C2).astype(F32)
        n = normed(x)
        own = x[2 * FRAMES * GROUP :]
        kv = jnp.dot(n, w_kv[...], preferred_element_type=F32)
        q = jnp.dot(n[2 * FRAMES * GROUP :], w_q[...], preferred_element_type=F32) * (1.0 / 16.0)
        qs = halves(q, FRAMES)
        ks = halves(kv[:, :C2], 3 * FRAMES)
        vs = halves(kv[:, C2:], 3 * FRAMES)
        pad = jnp.zeros((KEYS_PAD - KEYS, C2), BF16)
        attended = []
        for h in range(2):
            k = jnp.concatenate([ks[h], pad], axis=0)
            v = jnp.concatenate([vs[h], pad], axis=0)
            scores = lax.dot_general(qs[h], k, (((1,), (1,)), ((), ())), preferred_element_type=F32)
            scores = jnp.minimum(scores, bound[...])
            top = jnp.max(scores, axis=-1, keepdims=True)
            e = jnp.exp(scores - top)
            total = jnp.sum(e, axis=-1, keepdims=True)
            o = jnp.dot(e.astype(BF16), v, preferred_element_type=F32) / total
            attended.append(o.reshape(FRAMES, 1, 8, C2))
        a = jnp.concatenate(attended, axis=1).reshape(FRAMES * GROUP, C2).astype(BF16)
        result = own + jnp.dot(a, w_o[...], preferred_element_type=F32)
        frame = lax.broadcasted_iota(jnp.int32, (FRAMES * GROUP, C2), 0) // GROUP
        result = jnp.where(frame < valid, result, 0.0)
        out[:, 0, at, :] = result.astype(BF16).reshape(FRAMES, GROUP, C2)
        return 0

    lax.fori_loop(0, HALF // GROUP, block, 0)


def attend(info, lat, one, two, w_q, w_kv, w_o):
    vm = pl.BlockSpec(memory_space=pltpu.VMEM)
    return pl.pallas_call(
        functools.partial(attend_kernel, 0),
        out_shape=jax.ShapeDtypeStruct((FRAMES, 1, HALF, C2), BF16),
        in_specs=[pl.BlockSpec(memory_space=pltpu.SMEM)] + [vm] * 9,
        out_specs=vm,
        scratch_shapes=[pltpu.VMEM((ROWS, KEYS_PAD), F32)],
        compiler_params=pltpu.CompilerParams(vmem_limit_bytes=48 * 2**20),
        name="attend",
    )(info, *lat, *one, *two, w_q, w_kv, w_o)


def conv_weights(w):
    zero = jnp.zeros((C1, C1), w.dtype)
    columns = []
    for b in range(3):
        for r in range(2):
            columns.append(jnp.concatenate([w[i - r, b] if 0 <= i - r <= 2 else zero for i in range(4)], axis=0))
    return jnp.concatenate(columns, axis=1)


def time_weights(w):
    zero = jnp.zeros((C1, C1), w.dtype)
    left = jnp.concatenate([w[0], zero, w[1], zero, w[2], zero], axis=0)
    right = jnp.concatenate([zero, w[0], zero, w[1], zero, w[2]], axis=0)
    return jnp.concatenate([left, right], axis=1)


SPLIT = 9


def local(video, clip_table, w_spatial, w_temporal, w_down, w_query, w_key, w_value, w_out):
    position = lax.axis_index("stretch")
    ends = jnp.cumsum(clip_table[0])
    starts = ends - clip_table[0]
    member = (starts <= position) & (position < ends)
    offset = jnp.sum(jnp.where(member, position - starts, 0))
    is_last = member & (ends - 1 == position)
    valid = jnp.where(jnp.any(is_last), jnp.sum(jnp.where(is_last, clip_table[1], 0)), FRAMES)
    info = jnp.stack([offset, valid]).astype(jnp.int32)

    conv_at = SPLIT - 2
    up_a = send(video[conv_at:, 1], "tile", 1)
    down_a = send(video[conv_at:, 0], "tile", -1)
    up_b = send(video[:conv_at, 1], "tile", 1)
    down_b = send(video[:conv_at, 0], "tile", -1)
    w_c = conv_weights(w_spatial)
    w_t = time_weights(w_temporal)
    w_kv = jnp.concatenate([w_key, w_value], axis=1)

    lat_a, planes = front_a(video, up_a, down_a, w_c, w_t, w_down, conv_at)
    tail = send(planes[2:], "stretch", 1)
    one_a = send(lat_a, "stretch", 1)
    two_a = send(lat_a, "stretch", 2)
    lat_b = front_b(video, up_b, down_b, tail, planes, info, w_c, w_t, w_down, conv_at)
    one_b = send(lat_b, "stretch", 1)
    two_b = send(lat_b, "stretch", 2)
    return attend(info, (lat_b, lat_a), (one_b, one_a), (two_b, two_a), w_query, w_kv, w_out)


def solution(mesh):
    in_specs = (P("stretch", "tile", None, None), P(), P(), P(), P(), P(), P(), P(), P())
    out_specs = P("stretch", "tile", None, None)
    return jax.shard_map(local, mesh=mesh, in_specs=in_specs, out_specs=out_specs, check_vma=False)
```

```python
import functools

import jax
import jax.numpy as jnp
from jax import lax
from jax.experimental import pallas as pl
from jax.experimental.pallas import tpu as pltpu
from jax.sharding import PartitionSpec as P

F32 = jnp.float32
BF16 = jnp.bfloat16
FRAMES = 17
COLS = 320
HALF = 160
C1 = 128
C2 = 256
GROUP = 16
BIG = 3.0e38


def shift_perm(axis, by):
    count = lax.axis_size(axis)
    return [(i, i + by) for i in range(count) if 0 <= i + by < count]


def send(x, axis, by):
    return lax.ppermute(x, axis, shift_perm(axis, by))


def spread_weights(w_conv, w_time, conv, time):
    zero = jnp.zeros((C1, C1), BF16)
    for b in range(3):
        for r in range(2):
            at = slice((2 * b + r) * C1, (2 * b + r + 1) * C1)
            for i in range(4):
                conv[i * C1 : (i + 1) * C1, at] = w_conv[i - r, b] if 0 <= i - r <= 2 else zero
    for i in range(3):
        for r in range(2):
            for c in range(2):
                block = w_time[i] if r == c else zero
                time[(2 * i + r) * C1 : (2 * i + r + 1) * C1, c * C1 : (c + 1) * C1] = block


def conv_frames(count, at, vid, up, down, w_conv, planes):
    row = lax.broadcasted_iota(jnp.int32, (COLS, 2 * C1), 0)
    for f in range(count):
        x = jnp.concatenate([up[f], vid[f, 0], vid[f, 1], down[f]], axis=1)
        y = jnp.dot(x, w_conv[...], preferred_element_type=F32)
        left = pltpu.roll(y[:, : 2 * C1], 1, 0)
        right = pltpu.roll(y[:, 4 * C1 :], COLS - 1, 0)
        plane = (
            y[:, 2 * C1 : 4 * C1]
            + jnp.where(row == 0, 0.0, left)
            + jnp.where(row == COLS - 1, 0.0, right)
        )
        planes[f + at] = plane.astype(BF16)


def latent_frames(frames, at, vid, planes, mixed, bands, w_time, w_down, latent):
    for g in frames:
        f = g + at
        m_ref = mixed.at[g % 4]
        x = jnp.concatenate([planes[g], planes[g + 1], planes[g + 2]], axis=1)
        v = jnp.dot(x, w_time[...], preferred_element_type=F32)
        gate = v * (0.5 * jnp.tanh(0.5 * v) + 0.5)
        residual = jnp.concatenate([vid[f, 0], vid[f, 1]], axis=1).astype(F32)
        m = residual + gate
        m_ref[0:COLS, :] = m[:, :C1]
        m_ref[COLS:, :] = m[:, C1:]
        p = m_ref[pl.ds(0, HALF, stride=2), :]
        q = m_ref[pl.ds(1, HALF, stride=2), :]
        r = m_ref[pl.ds(COLS, HALF, stride=2), :]
        s = m_ref[pl.ds(COLS + 1, HALF, stride=2), :]
        top, low = p + q, r + s
        top_d, low_d = p - q, r - s
        b = jnp.concatenate([top + low, top_d + low_d, top - low, top_d - low_d], axis=1)
        bands[g * HALF : (g + 1) * HALF] = (b * 0.5).astype(BF16)
    first, last = frames[0], frames[-1] + 1
    out = jnp.dot(bands[first * HALF : last * HALF], w_down[...], preferred_element_type=F32)
    latent[first:last] = out.astype(BF16).reshape(last - first, HALF, C2)


def front_a_kernel(first, count, video, up, down, w_conv, w_time, w_down,
                   latent, context, tail, vid, planes, mixed, bands, conv, time, sems):
    copy = pltpu.make_async_copy(video.at[pl.ds(first, count)], vid, sems.at[0])
    copy.start()
    spread_weights(w_conv, w_time, conv, time)
    copy.wait()
    conv_frames(count, 0, vid, up, down, conv, planes)
    context[...] = planes[0:2]
    tail[...] = planes[count - 2 : count]
    latent_frames(range(count - 2), 2, vid, planes, mixed, bands, time, w_down, latent)


def front_scratch(frames, planes):
    return [
        pltpu.VMEM((frames, 2, COLS, C1), BF16),
        pltpu.VMEM((planes, COLS, 2 * C1), BF16),
        pltpu.VMEM((4, 2 * COLS, C1), F32),
        pltpu.VMEM((frames * HALF, 4 * C1), BF16),
        pltpu.VMEM((4 * C1, 6 * C1), BF16),
        pltpu.VMEM((6 * C1, 2 * C1), BF16),
        pltpu.SemaphoreType.DMA((1,)),
    ]


def front_cost(frames, latents):
    flops = 2 * COLS * (frames * 512 * 768 + latents * 768 * 256) + 2 * latents * HALF * 512 * 256
    moved = 2 * C1 * COLS * (4 * frames + latents)
    return pl.CostEstimate(flops=flops, bytes_accessed=2 * moved, transcendentals=0)


def front_a(video, up, down, w_conv, w_time, w_down, first):
    count = FRAMES - first
    vm = pl.BlockSpec(memory_space=pltpu.VMEM)
    two = jax.ShapeDtypeStruct((2, COLS, 2 * C1), BF16)
    return pl.pallas_call(
        functools.partial(front_a_kernel, first, count),
        out_shape=(jax.ShapeDtypeStruct((count - 2, HALF, C2), BF16), two, two),
        in_specs=[pl.BlockSpec(memory_space=pl.ANY)] + [vm] * 5,
        out_specs=(vm, vm, vm),
        scratch_shapes=front_scratch(count, count),
        compiler_params=pltpu.CompilerParams(vmem_limit_bytes=48 * 2**20),
        cost_estimate=front_cost(count, count - 2),
        name="front_a",
    )(video, up, down, w_conv, w_time, w_down)


def front_b_kernel(count, offset, video, up, down, tail, after, w_conv, w_time, w_down,
                   latent, vid, planes, mixed, bands, conv, time, sems):
    copy = pltpu.make_async_copy(video.at[pl.ds(0, count + 2)], vid, sems.at[0])
    copy.start()
    spread_weights(w_conv, w_time, conv, time)
    planes[count + 2 : count + 4] = after[...]
    copy.wait()
    conv_frames(count, 2, vid, up, down, conv, planes)
    is_start = offset[0] == 0

    @pl.when(is_start)
    def _():
        planes[0] = planes[2]
        planes[1] = planes[2]

    @pl.when(jnp.logical_not(is_start))
    def _():
        planes[0:2] = tail[...]

    latent_frames(range(count + 2), 0, vid, planes, mixed, bands, time, w_down, latent)


def front_b(video, up, down, tail, after, offset, w_conv, w_time, w_down, count):
    vm = pl.BlockSpec(memory_space=pltpu.VMEM)
    return pl.pallas_call(
        functools.partial(front_b_kernel, count),
        out_shape=jax.ShapeDtypeStruct((count + 2, HALF, C2), BF16),
        in_specs=[pl.BlockSpec(memory_space=pltpu.SMEM), pl.BlockSpec(memory_space=pl.ANY)] + [vm] * 7,
        out_specs=vm,
        scratch_shapes=front_scratch(count + 2, count + 4),
        compiler_params=pltpu.CompilerParams(vmem_limit_bytes=48 * 2**20),
        cost_estimate=front_cost(count, count + 2),
        name="front_b",
    )(offset, video, up, down, tail, after, w_conv, w_time, w_down)


KEYS = 3 * FRAMES * 8
KEYS_PAD = 512
ROWS = FRAMES * 8


def attend_kernel(split, info, lat_b, lat_a, one_b, one_a, two_b, two_a, w_q, w_kv, w_o, out, bound):
    offset = info[0]
    valid = info[1]
    r = lax.broadcasted_iota(jnp.int32, (ROWS, KEYS_PAD), 0)
    c = lax.broadcasted_iota(jnp.int32, (ROWS, KEYS_PAD), 1)
    same = jnp.bitwise_and(r, 7) == jnp.bitwise_and(c, 7)
    t = jnp.right_shift(r, 3)
    s = jnp.right_shift(c, 3)
    low = jnp.where(offset >= 2, 0, jnp.where(offset == 1, FRAMES, 2 * FRAMES))
    allowed = same & (s >= low) & (s <= t + 2 * FRAMES)
    bound[...] = jnp.where(allowed, BIG, -1e30)

    def normed(x):
        return (x * lax.rsqrt(jnp.mean(x * x, axis=-1, keepdims=True) + 1e-6)).astype(BF16)

    def halves(x, frames):
        x = x.reshape(frames, 2, 8, C2)
        return [x[:, h].reshape(frames * 8, C2).astype(BF16) for h in range(2)]

    def block(g, _):
        at = pl.ds(pl.multiple_of(g * GROUP, GROUP), GROUP)
        parts = [two_b, two_a, one_b, one_a, lat_b, lat_a]
        x = jnp.concatenate([p[:, at, :] for p in parts], axis=0)
        x = x.reshape(3 * FRAMES * GROUP, C2).astype(F32)
        n = normed(x)
        own = x[2 * FRAMES * GROUP :]
        kv = jnp.dot(n, w_kv[...], preferred_element_type=F32)
        q = jnp.dot(n[2 * FRAMES * GROUP :], w_q[...], preferred_element_type=F32) * (1.0 / 16.0)
        qs = halves(q, FRAMES)
        ks = halves(kv[:, :C2], 3 * FRAMES)
        vs = halves(kv[:, C2:], 3 * FRAMES)
        pad = jnp.zeros((KEYS_PAD - KEYS, C2), BF16)
        attended = []
        for h in range(2):
            k = jnp.concatenate([ks[h], pad], axis=0)
            v = jnp.concatenate([vs[h], pad], axis=0)
            scores = lax.dot_general(qs[h], k, (((1,), (1,)), ((), ())), preferred_element_type=F32)
            scores = jnp.minimum(scores, bound[...])
            top = jnp.max(scores, axis=-1, keepdims=True)
            e = jnp.exp(scores - top)
            total = jnp.sum(e, axis=-1, keepdims=True)
            o = jnp.dot(e.astype(BF16), v, preferred_element_type=F32) / total
            attended.append(o.reshape(FRAMES, 1, 8, C2))
        a = jnp.concatenate(attended, axis=1).reshape(FRAMES * GROUP, C2).astype(BF16)
        result = own + jnp.dot(a, w_o[...], preferred_element_type=F32)
        frame = lax.broadcasted_iota(jnp.int32, (FRAMES * GROUP, C2), 0) // GROUP
        result = jnp.where(frame < valid, result, 0.0)
        out[:, 0, at, :] = result.astype(BF16).reshape(FRAMES, GROUP, C2)
        return 0

    lax.fori_loop(0, HALF // GROUP, block, 0, unroll=2)


def attend(info, lat, one, two, w_q, w_kv, w_o):
    vm = pl.BlockSpec(memory_space=pltpu.VMEM)
    return pl.pallas_call(
        functools.partial(attend_kernel, 0),
        out_shape=jax.ShapeDtypeStruct((FRAMES, 1, HALF, C2), BF16),
        in_specs=[pl.BlockSpec(memory_space=pltpu.SMEM)] + [vm] * 9,
        out_specs=vm,
        scratch_shapes=[pltpu.VMEM((ROWS, KEYS_PAD), F32)],
        compiler_params=pltpu.CompilerParams(vmem_limit_bytes=48 * 2**20),
        name="attend",
    )(info, *lat, *one, *two, w_q, w_kv, w_o)


BACK_FRAMES = 10


def back_hops(count, ring):
    first = [(s, s + ring - 1 if s % ring == 0 else s - 1) for s in range(count - 2)]
    first = [(i, j) for i, j in first if j < count]
    return first, [(j, i + 2) for i, j in first]


def local(video, clip_table, w_spatial, w_temporal, w_down, w_query, w_key, w_value, w_out):
    position = lax.axis_index("stretch")
    ends = jnp.cumsum(clip_table[0])
    starts = ends - clip_table[0]
    member = (starts <= position) & (position < ends)
    offset = jnp.sum(jnp.where(member, position - starts, 0))
    is_last = member & (ends - 1 == position)
    valid = jnp.where(jnp.any(is_last), jnp.sum(jnp.where(is_last, clip_table[1], 0)), FRAMES)
    info = jnp.stack([offset, valid]).astype(jnp.int32)

    conv_at = FRAMES - BACK_FRAMES - 2
    up_a = send(video[conv_at:, 1], "tile", 1)
    down_a = send(video[conv_at:, 0], "tile", -1)
    up_b = send(video[:conv_at, 1], "tile", 1)
    down_b = send(video[:conv_at, 0], "tile", -1)
    w_kv = jnp.concatenate([w_key, w_value], axis=1)
    hop, hop_on = back_hops(lax.axis_size("stretch"), 4)

    lat_a, context, tail = front_a(video, up_a, down_a, w_spatial, w_temporal, w_down, conv_at)
    tail = send(tail, "stretch", 1)
    back = lax.ppermute(lat_a, "stretch", hop)
    one_a = send(lat_a, "stretch", 1)
    lat_b = front_b(video, up_b, down_b, tail, context, info, w_spatial, w_temporal, w_down, conv_at)
    two_b = send(lat_b, "stretch", 2)
    one_b = send(lat_b, "stretch", 1)
    two_a = lax.ppermute(back, "stretch", hop_on)
    return attend(info, (lat_b, lat_a), (one_b, one_a), (two_b, two_a), w_query, w_kv, w_out)


def solution(mesh):
    in_specs = (P("stretch", "tile", None, None), P(), P(), P(), P(), P(), P(), P(), P())
    out_specs = P("stretch", "tile", None, None)
    return jax.shard_map(local, mesh=mesh, in_specs=in_specs, out_specs=out_specs, check_vma=False)
```

```python
import functools

import jax
import jax.numpy as jnp
from jax import lax
from jax.experimental import pallas as pl
from jax.experimental.pallas import tpu as pltpu
from jax.sharding import PartitionSpec as P

F32 = jnp.float32
BF16 = jnp.bfloat16
FRAMES = 17
COLS = 320
HALF = 160
C1 = 128
C2 = 256
BIG = 3.0e38
VM = pl.BlockSpec(memory_space=pltpu.VMEM)
SM = pl.BlockSpec(memory_space=pltpu.SMEM)
VMEM_EDGES = 60 * 2**20
VMEM_FRONT = 28 * 2**20
VMEM_ATTEND = 24 * 2**20


def shift_perm(axis, by):
    count = lax.axis_size(axis)
    return [(i, i + by) for i in range(count) if 0 <= i + by < count]


def send(x, axis, by):
    return lax.ppermute(x, axis, shift_perm(axis, by))


def spread_weights(w_conv, w_time, conv, time):
    zero = jnp.zeros((C1, C1), BF16)
    for b in range(3):
        for r in range(2):
            at = slice((2 * b + r) * C1, (2 * b + r + 1) * C1)
            for i in range(4):
                conv[i * C1 : (i + 1) * C1, at] = w_conv[i - r, b] if 0 <= i - r <= 2 else zero
    for i in range(3):
        for r in range(2):
            for c in range(2):
                block = w_time[i] if r == c else zero
                time[(2 * i + r) * C1 : (2 * i + r + 1) * C1, c * C1 : (c + 1) * C1] = block


def edge_kernel(video, low, high, last, last_low, last_high, sems):
    end = pl.ds(FRAMES - 2, 2)
    pairs = [
        (video.at[:, 1], low),
        (video.at[:, 0], high),
        (video.at[end], last),
        (video.at[end, 1], last_low),
        (video.at[end, 0], last_high),
    ]
    copies = [pltpu.make_async_copy(*pair, sems.at[i]) for i, pair in enumerate(pairs)]
    for copy in copies:
        copy.start()
    for copy in copies:
        copy.wait()


def edges(video):
    row = jax.ShapeDtypeStruct((FRAMES, COLS, C1), BF16)
    last_row = jax.ShapeDtypeStruct((2, COLS, C1), BF16)
    return pl.pallas_call(
        edge_kernel,
        out_shape=(row, row, jax.ShapeDtypeStruct((2, 2, COLS, C1), BF16), last_row, last_row),
        in_specs=[pl.BlockSpec(memory_space=pl.ANY)],
        out_specs=(VM,) * 5,
        scratch_shapes=[pltpu.SemaphoreType.DMA((5,))],
        compiler_params=pltpu.CompilerParams(vmem_limit_bytes=VMEM_EDGES),
        name="edges",
    )(video)


def weights_kernel(w_conv, w_time, w_down, conv, time, down):
    spread_weights(w_conv, w_time, conv, time)
    down[...] = w_down[...]


def front_weights(w_conv, w_time, w_down):
    return pl.pallas_call(
        weights_kernel,
        out_shape=(
            jax.ShapeDtypeStruct((4 * C1, 6 * C1), BF16),
            jax.ShapeDtypeStruct((6 * C1, 2 * C1), BF16),
            jax.ShapeDtypeStruct((4 * C1, C2), BF16),
        ),
        in_specs=[VM] * 3,
        out_specs=(VM, VM, VM),
        compiler_params=pltpu.CompilerParams(vmem_limit_bytes=VMEM_FRONT),
        name="front_weights",
    )(w_conv, w_time, w_down)


def conv_frames(count, at, vid, up, down, w_conv, planes):
    row = lax.broadcasted_iota(jnp.int32, (COLS, 2 * C1), 0)
    for f in range(count):
        x = jnp.concatenate([up[f], vid[f, 0], vid[f, 1], down[f]], axis=1)
        y = jnp.dot(x, w_conv[...], preferred_element_type=F32)
        left = pltpu.roll(y[:, : 2 * C1], 1, 0)
        right = pltpu.roll(y[:, 4 * C1 :], COLS - 1, 0)
        plane = (
            y[:, 2 * C1 : 4 * C1]
            + jnp.where(row == 0, 0.0, left)
            + jnp.where(row == COLS - 1, 0.0, right)
        )
        planes[f + at] = plane.astype(BF16)


def latent_frames(vid, planes, mixed, bands, w_time, w_down, latents):
    for g in range(FRAMES):
        m_ref = mixed.at[g % 4]
        x = jnp.concatenate([planes[g], planes[g + 1], planes[g + 2]], axis=1)
        v = jnp.dot(x, w_time[...], preferred_element_type=F32)
        gate = v * (0.5 * jnp.tanh(0.5 * v) + 0.5)
        residual = jnp.concatenate([vid[g, 0], vid[g, 1]], axis=1).astype(F32)
        m = residual + gate
        m_ref[0:COLS, :] = m[:, :C1]
        m_ref[COLS:, :] = m[:, C1:]
        p = m_ref[pl.ds(0, HALF, stride=2), :]
        q = m_ref[pl.ds(1, HALF, stride=2), :]
        r = m_ref[pl.ds(COLS, HALF, stride=2), :]
        s = m_ref[pl.ds(COLS + 1, HALF, stride=2), :]
        top, low = p + q, r + s
        top_d, low_d = p - q, r - s
        b = jnp.concatenate([top + low, top_d + low_d, top - low, top_d - low_d], axis=1)
        bands[g * HALF : (g + 1) * HALF] = (b * 0.5).astype(BF16)
    at = 0
    for latent in latents:
        frames = latent.shape[0]
        x = bands[at * HALF : (at + frames) * HALF]
        out = jnp.dot(x, w_down[...], preferred_element_type=F32)
        latent[...] = out.astype(BF16).reshape(frames, HALF, C2)
        at += frames


def front_kernel(info, video, up, down, before, before_up, before_down, w_conv, w_time, w_down,
                 lat_b, lat_a, planes, mixed, bands):
    conv_frames(2, 0, before, before_up, before_down, w_conv, planes)
    conv_frames(FRAMES, 2, video, up, down, w_conv, planes)

    @pl.when(info[0] == 0)
    def _():
        planes[0] = planes[2]
        planes[1] = planes[2]

    latent_frames(video, planes, mixed, bands, w_time, w_down, (lat_b, lat_a))


def front(info, video, up, down, before, before_up, before_down, w_conv, w_time, w_down):
    return pl.pallas_call(
        front_kernel,
        out_shape=(
            jax.ShapeDtypeStruct((FRAMES - BACK_FRAMES, HALF, C2), BF16),
            jax.ShapeDtypeStruct((BACK_FRAMES, HALF, C2), BF16),
        ),
        in_specs=[SM] + [VM] * 9,
        out_specs=(VM, VM),
        scratch_shapes=[
            pltpu.VMEM((FRAMES + 2, COLS, 2 * C1), BF16),
            pltpu.VMEM((4, 2 * COLS, C1), F32),
            pltpu.VMEM((FRAMES * HALF, 4 * C1), BF16),
        ],
        compiler_params=pltpu.CompilerParams(vmem_limit_bytes=VMEM_FRONT),
        name="front",
    )(info, video, up, down, before, before_up, before_down, w_conv, w_time, w_down)


ROWS = FRAMES * 8
KEYS_PAD = 256
GROUPS = HALF // 8


def normalize(x):
    return (x * lax.rsqrt(jnp.mean(x * x, axis=-1, keepdims=True) + 1e-6)).astype(BF16)


def project(parts, weights, targets):
    at = 0
    for part in parts:
        frames = part.shape[0]
        for f0 in range(0, frames, 5):
            count = min(5, frames - f0)
            x = normalize(part[f0 : f0 + count].reshape(count * HALF, C2).astype(F32))
            for w, scale, target in zip(weights, (1.0, 1.0, 1.0 / 16.0), targets):
                y = jnp.dot(x, w[...], preferred_element_type=F32)
                if scale != 1.0:
                    y = y * scale
                y = y.reshape(count, GROUPS, 8, C2)
                for f in range(count):
                    target[:, (at + f0 + f) * 8 : (at + f0 + f + 1) * 8, :] = y[f]
        at += frames


def attend_group(q, k, v, bound):
    pad = jnp.zeros((KEYS_PAD - ROWS, C2), BF16)
    k = jnp.concatenate([k.astype(BF16), pad], axis=0)
    v = jnp.concatenate([v.astype(BF16), pad], axis=0)
    scores = lax.dot_general(q.astype(BF16), k, (((1,), (1,)), ((), ())), preferred_element_type=F32)
    scores = jnp.minimum(scores, bound[...])
    top = jnp.max(scores, axis=-1, keepdims=True)
    e = jnp.exp(scores - top)
    total = jnp.sum(e, axis=-1, keepdims=True)
    return top, total, jnp.dot(e.astype(BF16), v, preferred_element_type=F32)


def positions():
    r = lax.broadcasted_iota(jnp.int32, (ROWS, KEYS_PAD), 0)
    c = lax.broadcasted_iota(jnp.int32, (ROWS, KEYS_PAD), 1)
    same = jnp.bitwise_and(r, 7) == jnp.bitwise_and(c, 7)
    return same, jnp.right_shift(r, 3), jnp.right_shift(c, 3)


def attend_own_kernel(lat_b, lat_a, w_q, w_k, w_v, q_out, o_out, lse_out, ks, vs, bound):
    same, t, s = positions()
    bound[...] = jnp.where(same & (s <= t), BIG, -1e30)
    project((lat_b, lat_a), (w_k, w_v, w_q), (ks, vs, q_out))

    def group(g, _):
        top, total, o = attend_group(q_out[g], ks[g], vs[g], bound)
        o_out[g] = o / total
        lse_out[g] = jnp.broadcast_to(top + jnp.log(total), (ROWS, 128))
        return 0

    lax.fori_loop(0, GROUPS, group, 0, unroll=4)


def merge(top, total, o, o_before, lse_before):
    top = jnp.broadcast_to(top, lse_before.shape)
    total = jnp.broadcast_to(total, lse_before.shape)
    most = jnp.maximum(lse_before, top)
    old, new = jnp.exp(lse_before - most), jnp.exp(top - most)
    whole = old + total * new
    share = 1.0 / whole
    old, new = old * share, new * share
    o = o_before * jnp.concatenate([old, old], axis=1) + o * jnp.concatenate([new, new], axis=1)
    return o, most + jnp.log(whole)


def part_bound(info, parts, distances, bound):
    same, _, s = positions()
    offset = info[0]
    first = jnp.where(offset >= distances[0], 0, parts[0].shape[0])
    last = jnp.where(offset >= distances[1], FRAMES, parts[0].shape[0])
    bound[...] = jnp.where(same & (s >= first) & (s < last), BIG, -1e30)


def attend_more_kernel(distances, info, part0, part1, w_k, w_v, q_in, o_in, lse_in, o_out, lse_out, ks, vs, bound):
    part_bound(info, (part0, part1), distances, bound)
    project((part0, part1), (w_k, w_v), (ks, vs))

    def group(g, _):
        top, total, o = attend_group(q_in[g], ks[g], vs[g], bound)
        o, lse = merge(top, total, o, o_in[g], lse_in[g])
        o_out[g] = o
        lse_out[g] = lse
        return 0

    lax.fori_loop(0, GROUPS, group, 0, unroll=4)


def attend_last_kernel(distances, info, part0, part1, w_k, w_v, q_in, o_in, lse_in, lat_b, lat_a, w_o, out,
                       ks, vs, bound, attended):
    part_bound(info, (part0, part1), distances, bound)
    project((part0, part1), (w_k, w_v), (ks, vs))

    def group(g, _):
        top, total, o = attend_group(q_in[g], ks[g], vs[g], bound)
        o, _ = merge(top, total, o, o_in[g], lse_in[g])
        attended[:, pl.ds(pl.multiple_of(g * 8, 8), 8), :] = o.reshape(FRAMES, 8, C2)
        return 0

    lax.fori_loop(0, GROUPS, group, 0, unroll=4)
    valid = info[1]
    at = 0
    for part in (lat_b, lat_a):
        frames = part.shape[0]
        a = attended[at : at + frames].reshape(frames * HALF, C2).astype(BF16)
        update = jnp.dot(a, w_o[...], preferred_element_type=F32).reshape(frames, HALF, C2)
        for f in range(frames):
            value = part[f].astype(F32) + update[f]
            out[at + f, 0] = jnp.where(at + f < valid, value, 0.0).astype(BF16)
        at += frames


BY_GROUP = jax.ShapeDtypeStruct((GROUPS, ROWS, C2), F32)
BY_GROUP_LSE = jax.ShapeDtypeStruct((GROUPS, ROWS, 128), F32)
ATTEND_SCRATCH = [
    pltpu.VMEM((GROUPS, ROWS, C2), F32),
    pltpu.VMEM((GROUPS, ROWS, C2), F32),
    pltpu.VMEM((ROWS, KEYS_PAD), F32),
]
ATTEND_COST = pl.CostEstimate(flops=3 * 10**9, bytes_accessed=10**7, transcendentals=10**6)


def attend_own(lat_b, lat_a, w_q, w_k, w_v):
    return pl.pallas_call(
        attend_own_kernel,
        out_shape=(BY_GROUP, BY_GROUP, BY_GROUP_LSE),
        in_specs=[VM] * 5,
        out_specs=(VM, VM, VM),
        scratch_shapes=ATTEND_SCRATCH,
        compiler_params=pltpu.CompilerParams(vmem_limit_bytes=VMEM_ATTEND),
        cost_estimate=ATTEND_COST,
        name="attend_own",
    )(lat_b, lat_a, w_q, w_k, w_v)


def attend_more(distances, info, part0, part1, w_k, w_v, q, o, lse):
    return pl.pallas_call(
        functools.partial(attend_more_kernel, distances),
        out_shape=(BY_GROUP, BY_GROUP_LSE),
        in_specs=[SM] + [VM] * 7,
        out_specs=(VM, VM),
        scratch_shapes=ATTEND_SCRATCH,
        compiler_params=pltpu.CompilerParams(vmem_limit_bytes=VMEM_ATTEND),
        cost_estimate=ATTEND_COST,
        name="attend_more",
    )(info, part0, part1, w_k, w_v, q, o, lse)


def attend_last(distances, info, part0, part1, w_k, w_v, q, o, lse, lat_b, lat_a, w_o):
    return pl.pallas_call(
        functools.partial(attend_last_kernel, distances),
        out_shape=jax.ShapeDtypeStruct((FRAMES, 1, HALF, C2), BF16),
        in_specs=[SM] + [VM] * 10,
        out_specs=VM,
        scratch_shapes=ATTEND_SCRATCH + [pltpu.VMEM((FRAMES, HALF, C2), F32)],
        compiler_params=pltpu.CompilerParams(vmem_limit_bytes=VMEM_ATTEND),
        cost_estimate=ATTEND_COST,
        name="attend_last",
    )(info, part0, part1, w_k, w_v, q, o, lse, lat_b, lat_a, w_o)


BACK_FRAMES = 10


def next_stretch(by):
    stretches, tiles = lax.axis_size("stretch"), lax.axis_size("tile")
    return [
        (s * tiles + t, (s + 1) * tiles + t + by)
        for s in range(stretches - 1)
        for t in range(tiles)
        if 0 <= t + by < tiles
    ]


def back_hops(count, ring):
    first = [(s, s + ring - 1 if s % ring == 0 else s - 1) for s in range(count - 2)]
    first = [(i, j) for i, j in first if j < count]
    return first, [(j, i + 2) for i, j in first]


def local(video, clip_table, w_spatial, w_temporal, w_down, w_query, w_key, w_value, w_out):
    position = lax.axis_index("stretch")
    ends = jnp.cumsum(clip_table[0])
    starts = ends - clip_table[0]
    member = (starts <= position) & (position < ends)
    offset = jnp.sum(jnp.where(member, position - starts, 0))
    is_last = member & (ends - 1 == position)
    valid = jnp.where(jnp.any(is_last), jnp.sum(jnp.where(is_last, clip_table[1], 0)), FRAMES)
    info = jnp.stack([offset, valid]).astype(jnp.int32)

    low, high, last, last_low, last_high = edges(video)
    up = send(low, "tile", 1)
    down = send(high, "tile", -1)
    before = send(last, "stretch", 1)
    before_up = lax.ppermute(last_low, ("stretch", "tile"), next_stretch(1))
    before_down = lax.ppermute(last_high, ("stretch", "tile"), next_stretch(-1))
    weights = front_weights(w_spatial, w_temporal, w_down)
    hop, hop_on = back_hops(lax.axis_size("stretch"), 4)

    lat_b, lat_a = front(info, video, up, down, before, before_up, before_down, *weights)
    back = lax.ppermute(lat_a, "stretch", hop)
    one_b = send(lat_b, "stretch", 1)
    q, o, lse = attend_own(lat_b, lat_a, w_query, w_key, w_value)
    later, _ = lax.optimization_barrier((lat_a, lse))
    one_a = send(later, "stretch", 1)
    relay, _ = lax.optimization_barrier((one_b, lse))
    two_b = send(relay, "stretch", 1)
    back, _ = lax.optimization_barrier((back, lse))
    two_a = lax.ppermute(back, "stretch", hop_on)
    o, lse = attend_more((1, 1), info, one_b, one_a, w_key, w_value, q, o, lse)
    return attend_last((2, 2), info, two_b, two_a, w_key, w_value, q, o, lse, lat_b, lat_a, w_out)


def solution(mesh):
    in_specs = (P("stretch", "tile", None, None), P(), P(), P(), P(), P(), P(), P(), P())
    out_specs = P("stretch", "tile", None, None)
    return jax.shard_map(local, mesh=mesh, in_specs=in_specs, out_specs=out_specs, check_vma=False)
```

```python
import functools

import jax
import jax.numpy as jnp
from jax import lax
from jax.experimental import pallas as pl
from jax.experimental.pallas import tpu as pltpu
from jax.sharding import PartitionSpec as P

F32 = jnp.float32
BF16 = jnp.bfloat16
FRAMES = 17
COLS = 320
HALF = 160
C1 = 128
C2 = 256
BIG = 3.0e38
EDGE_STEP = 9
PARTS = (6, 11)
SMALL_COST = pl.CostEstimate(flops=10**6, bytes_accessed=10**4, transcendentals=0)
VM = pl.BlockSpec(memory_space=pltpu.VMEM)
SM = pl.BlockSpec(memory_space=pltpu.SMEM)
VMEM_EDGES = 60 * 2**20
VMEM_FRONT = 28 * 2**20
VMEM_ATTEND = 24 * 2**20


def shift_perm(axis, by):
    count = lax.axis_size(axis)
    return [(i, i + by) for i in range(count) if 0 <= i + by < count]


def send(x, axis, by):
    return lax.ppermute(x, axis, shift_perm(axis, by))


def spread_weights(w_conv, w_time, conv, time):
    zero = jnp.zeros((C1, C1), BF16)
    for b in range(3):
        for r in range(2):
            at = slice((2 * b + r) * C1, (2 * b + r + 1) * C1)
            for i in range(4):
                conv[i * C1 : (i + 1) * C1, at] = w_conv[i - r, b] if 0 <= i - r <= 2 else zero
    for i in range(3):
        for r in range(2):
            for c in range(2):
                block = w_time[i] * 0.5 if r == c else zero
                time[(2 * i + r) * C1 : (2 * i + r + 1) * C1, c * C1 : (c + 1) * C1] = block


def edge_kernel(video, low, high, last, last_low, last_high, sems):
    end = pl.ds(FRAMES - 2, 2)
    pairs = [
        (video.at[pl.ds(f, min(EDGE_STEP, FRAMES - f)), row], target.at[pl.ds(f, min(EDGE_STEP, FRAMES - f))])
        for row, target in ((1, low), (0, high))
        for f in range(0, FRAMES, EDGE_STEP)
    ]
    pairs += [
        (video.at[end], last),
        (video.at[end, 1], last_low),
        (video.at[end, 0], last_high),
    ]
    copies = [pltpu.make_async_copy(*pair, sems.at[i]) for i, pair in enumerate(pairs)]
    for copy in copies:
        copy.start()
    for copy in copies:
        copy.wait()


def edges(video):
    row = jax.ShapeDtypeStruct((FRAMES, COLS, C1), BF16)
    last_row = jax.ShapeDtypeStruct((2, COLS, C1), BF16)
    return pl.pallas_call(
        edge_kernel,
        out_shape=(row, row, jax.ShapeDtypeStruct((2, 2, COLS, C1), BF16), last_row, last_row),
        in_specs=[pl.BlockSpec(memory_space=pl.ANY)],
        out_specs=(VM,) * 5,
        scratch_shapes=[pltpu.SemaphoreType.DMA((3 + 2 * -(-FRAMES // EDGE_STEP),))],
        compiler_params=pltpu.CompilerParams(vmem_limit_bytes=VMEM_EDGES),
        cost_estimate=SMALL_COST,
        name="edges",
    )(video)


def weights_kernel(w_conv, w_time, w_down, conv, time, down):
    spread_weights(w_conv, w_time, conv, time)
    down[...] = w_down[...] * 0.5


def front_weights(w_conv, w_time, w_down):
    return pl.pallas_call(
        weights_kernel,
        out_shape=(
            jax.ShapeDtypeStruct((4 * C1, 6 * C1), BF16),
            jax.ShapeDtypeStruct((6 * C1, 2 * C1), BF16),
            jax.ShapeDtypeStruct((4 * C1, C2), BF16),
        ),
        in_specs=[VM] * 3,
        out_specs=(VM, VM, VM),
        compiler_params=pltpu.CompilerParams(vmem_limit_bytes=VMEM_FRONT),
        cost_estimate=SMALL_COST,
        name="front_weights",
    )(w_conv, w_time, w_down)


def conv_frames(first, at, count, vid, up, down, w_conv, planes):
    row = lax.broadcasted_iota(jnp.int32, (COLS, 2 * C1), 0)
    for f in range(count):
        g = first + f
        x = jnp.concatenate([up[g], vid[g, 0], vid[g, 1], down[g]], axis=1)
        y = jnp.dot(x, w_conv[...], preferred_element_type=F32)
        left = pltpu.roll(y[:, : 2 * C1], 1, 0)
        right = pltpu.roll(y[:, 4 * C1 :], COLS - 1, 0)
        plane = (
            y[:, 2 * C1 : 4 * C1]
            + jnp.where(row == 0, 0.0, left)
            + jnp.where(row == COLS - 1, 0.0, right)
        )
        planes[f + at] = plane.astype(BF16)


def latent_scratch(frames):
    return [pltpu.VMEM((4, 2 * COLS, C1), F32), pltpu.VMEM((frames * HALF, 4 * C1), BF16)]


def latent_frames(first, video, planes, mixed, bands, w_time, w_down, latent):
    frames = latent.shape[0]
    for g in range(frames):
        m_ref = mixed.at[g % 4]
        x = jnp.concatenate([planes[g], planes[g + 1], planes[g + 2]], axis=1)
        u = jnp.dot(x, w_time[...], preferred_element_type=F32)
        gate = u + u * jnp.tanh(u)
        residual = jnp.concatenate([video[first + g, 0], video[first + g, 1]], axis=1).astype(F32)
        m = residual + gate
        m_ref[0:COLS, :] = m[:, :C1]
        m_ref[COLS:, :] = m[:, C1:]
        p = m_ref[pl.ds(0, HALF, stride=2), :]
        q = m_ref[pl.ds(1, HALF, stride=2), :]
        r = m_ref[pl.ds(COLS, HALF, stride=2), :]
        s = m_ref[pl.ds(COLS + 1, HALF, stride=2), :]
        top, low = p + q, r + s
        top_d, low_d = p - q, r - s
        b = jnp.concatenate([top + low, top_d + low_d, top - low, top_d - low_d], axis=1)
        bands[g * HALF : (g + 1) * HALF] = b.astype(BF16)
    out = jnp.dot(bands[...], w_down[...], preferred_element_type=F32)
    latent[...] = out.astype(BF16).reshape(frames, HALF, C2)


def front_kernel(info, video, up, down, w_conv, w_time, w_down, latent, context, planes, mixed, bands):
    del info
    count = latent.shape[0]
    first = FRAMES - count
    conv_frames(0, 0, FRAMES, video, up, down, w_conv, planes)
    context[...] = planes[0:first]
    latent_frames(first, video, planes.at[pl.ds(first - 2, count + 2)], mixed, bands, w_time, w_down, latent)


def front(info, video, up, down, w_conv, w_time, w_down):
    first, count = PARTS
    return pl.pallas_call(
        front_kernel,
        out_shape=(
            jax.ShapeDtypeStruct((count, HALF, C2), BF16),
            jax.ShapeDtypeStruct((first, COLS, 2 * C1), BF16),
        ),
        in_specs=[SM] + [VM] * 6,
        out_specs=(VM,) * 2,
        scratch_shapes=[pltpu.VMEM((FRAMES, COLS, 2 * C1), BF16)] + latent_scratch(count),
        compiler_params=pltpu.CompilerParams(vmem_limit_bytes=VMEM_FRONT),
        cost_estimate=pl.CostEstimate(flops=29900000000, bytes_accessed=10**4, transcendentals=0),
        name="front",
    )(info, video, up, down, w_conv, w_time, w_down)


def front_first_kernel(info, video, before, before_up, before_down, context, w_conv, w_time, w_down,
                       latent, planes, mixed, bands):
    count = latent.shape[0]
    conv_frames(0, 0, 2, before, before_up, before_down, w_conv, planes)
    for f in range(2):
        planes[f] = jnp.where(info[0] == 0, context[0], planes[f])
    planes[2 : count + 2] = context[...]
    latent_frames(0, video, planes, mixed, bands, w_time, w_down, latent)


def front_first(info, video, before, before_up, before_down, context, w_conv, w_time, w_down):
    count = PARTS[0]
    return pl.pallas_call(
        front_first_kernel,
        out_shape=jax.ShapeDtypeStruct((count, HALF, C2), BF16),
        in_specs=[SM] + [VM] * 8,
        out_specs=VM,
        scratch_shapes=[pltpu.VMEM((count + 2, COLS, 2 * C1), BF16)] + latent_scratch(count),
        compiler_params=pltpu.CompilerParams(vmem_limit_bytes=VMEM_FRONT),
        cost_estimate=pl.CostEstimate(flops=4600000000, bytes_accessed=10**4, transcendentals=0),
        name="front_first",
    )(info, video, before, before_up, before_down, context, w_conv, w_time, w_down)


ROWS = FRAMES * 8
GROUPS = HALF // 8


def padded(frames):
    return -(-frames * 8 // 128) * 128


def normalize(x):
    return (x * lax.rsqrt(jnp.mean(x * x, axis=-1, keepdims=True) + 1e-6)).astype(BF16)


def project(parts, weights, targets):
    at = 0
    for part in parts:
        for f0 in range(0, part.shape[0], 6):
            frames = min(6, part.shape[0] - f0)
            x = normalize(part[f0 : f0 + frames].reshape(frames * HALF, C2).astype(F32))
            for w, scale, target in zip(weights, (1.0, 1.0, 1.0 / 16.0), targets):
                y = jnp.dot(x, w[...], preferred_element_type=F32)
                if scale != 1.0:
                    y = y * scale
                y = y.reshape(frames, GROUPS, 8, C2)
                for f in range(frames):
                    target[:, (at + f) * 8 : (at + f + 1) * 8, :] = y[f]
            at += frames


def attend_group(q, k, v, bound):
    pad = jnp.zeros((bound.shape[1] - k.shape[0], C2), BF16)
    k = jnp.concatenate([k.astype(BF16), pad], axis=0)
    v = jnp.concatenate([v.astype(BF16), pad], axis=0)
    scores = lax.dot_general(q.astype(BF16), k, (((1,), (1,)), ((), ())), preferred_element_type=F32)
    scores = jnp.minimum(scores, bound[...])
    top = jnp.max(scores, axis=-1, keepdims=True)
    e = jnp.exp(scores - top)
    total = jnp.sum(e, axis=-1, keepdims=True)
    return top, total, jnp.dot(e.astype(BF16), v, preferred_element_type=F32)


def positions(bound):
    r = lax.broadcasted_iota(jnp.int32, bound.shape, 0)
    c = lax.broadcasted_iota(jnp.int32, bound.shape, 1)
    same = jnp.bitwise_and(r, 7) == jnp.bitwise_and(c, 7)
    return same, jnp.right_shift(r, 3), jnp.right_shift(c, 3)


def attend_own_kernel(lat_0, lat_1, w_q, w_k, w_v, q_out, o_out, lse_out, ks, vs, bound):
    same, t, s = positions(bound)
    bound[...] = jnp.where(same & (s <= t), BIG, -1e30)
    project((lat_0, lat_1), (w_k, w_v, w_q), (ks, vs, q_out))

    def group(g, _):
        top, total, o = attend_group(q_out[g], ks[g], vs[g], bound)
        o_out[g] = o / total
        lse_out[g] = jnp.broadcast_to(top + jnp.log(total), (ROWS, 128))
        return 0

    lax.fori_loop(0, GROUPS, group, 0, unroll=10)


def merge(top, total, o, o_before, lse_before):
    top = jnp.broadcast_to(top, lse_before.shape)
    total = jnp.broadcast_to(total, lse_before.shape)
    most = jnp.maximum(lse_before, top)
    old, new = jnp.exp(lse_before - most), jnp.exp(top - most)
    whole = old + total * new
    share = 1.0 / whole
    old, new = old * share, new * share
    o = o_before * jnp.concatenate([old, old], axis=1) + o * jnp.concatenate([new, new], axis=1)
    return o, most + jnp.log(whole)


def part_bound(info, parts, distances, bound):
    same, _, s = positions(bound)
    offset = info[0]
    allowed = jnp.zeros(bound.shape, jnp.bool_)
    at = 0
    for part, distance in zip(parts, distances):
        end = at + part.shape[0]
        first = jnp.where(offset >= distance, at, end)
        allowed = allowed | ((s >= first) & (s < end))
        at = end
    bound[...] = jnp.where(same & allowed, BIG, -1e30)


def attend_more_kernel(distances, info, *refs):
    parts, refs = refs[: len(distances)], refs[len(distances) :]
    w_k, w_v, q_in, o_in, lse_in, o_out, lse_out, ks, vs, bound = refs
    part_bound(info, parts, distances, bound)
    project(parts, (w_k, w_v), (ks, vs))

    def group(g, _):
        top, total, o = attend_group(q_in[g], ks[g], vs[g], bound)
        o, lse = merge(top, total, o, o_in[g], lse_in[g])
        o_out[g] = o
        lse_out[g] = lse
        return 0

    lax.fori_loop(0, GROUPS, group, 0, unroll=10)


def attend_last_kernel(distances, info, *refs):
    parts, refs = refs[: len(distances)], refs[len(distances) :]
    w_k, w_v, q_in, o_in, lse_in, lat_0, lat_1, w_o, out, ks, vs, bound, attended, staged, sems = refs
    part_bound(info, parts, distances, bound)
    project(parts, (w_k, w_v), (ks, vs))

    def group(g, _):
        top, total, o = attend_group(q_in[g], ks[g], vs[g], bound)
        o, _ = merge(top, total, o, o_in[g], lse_in[g])
        attended[:, pl.ds(pl.multiple_of(g * 8, 8), 8), :] = o.reshape(FRAMES, 8, C2)
        return 0

    lax.fori_loop(0, GROUPS, group, 0, unroll=10)
    valid = info[1]
    at = 0
    copies = []
    for part in (lat_0, lat_1):
        for f0 in range(0, part.shape[0], 6):
            frames = min(6, part.shape[0] - f0)
            a = attended[at : at + frames].reshape(frames * HALF, C2).astype(BF16)
            update = jnp.dot(a, w_o[...], preferred_element_type=F32).reshape(frames, HALF, C2)
            for f in range(frames):
                value = part[f0 + f].astype(F32) + update[f]
                staged[at + f] = jnp.where(at + f < valid, value, 0.0).astype(BF16)
            done = pl.ds(at, frames)
            copies.append(pltpu.make_async_copy(staged.at[done], out.at[done, 0], sems.at[len(copies)]))
            copies[-1].start()
            at += frames
    for copy in copies:
        copy.wait()


BY_GROUP = jax.ShapeDtypeStruct((GROUPS, ROWS, C2), F32)
BY_GROUP_LSE = jax.ShapeDtypeStruct((GROUPS, ROWS, 128), F32)


def attend_scratch(parts):
    frames = sum(part.shape[0] for part in parts)
    return [
        pltpu.VMEM((GROUPS, frames * 8, C2), F32),
        pltpu.VMEM((GROUPS, frames * 8, C2), F32),
        pltpu.VMEM((ROWS, padded(frames)), F32),
    ]


def attend_own(lats, w_q, w_k, w_v):
    return pl.pallas_call(
        attend_own_kernel,
        out_shape=(BY_GROUP, BY_GROUP, BY_GROUP_LSE),
        in_specs=[VM] * 5,
        out_specs=(VM, VM, VM),
        scratch_shapes=attend_scratch(lats),
        compiler_params=pltpu.CompilerParams(vmem_limit_bytes=VMEM_ATTEND),
        cost_estimate=pl.CostEstimate(flops=4600000000, bytes_accessed=10**4, transcendentals=0),
        name="attend_own",
    )(*lats, w_q, w_k, w_v)


def attend_more(distances, info, parts, w_k, w_v, q, o, lse):
    return pl.pallas_call(
        functools.partial(attend_more_kernel, distances),
        out_shape=(BY_GROUP, BY_GROUP_LSE),
        in_specs=[SM] + [VM] * (len(parts) + 5),
        out_specs=(VM, VM),
        scratch_shapes=attend_scratch(parts),
        compiler_params=pltpu.CompilerParams(vmem_limit_bytes=VMEM_ATTEND),
        cost_estimate=pl.CostEstimate(flops=11500000, bytes_accessed=10**4, transcendentals=0),
        name="attend_more",
    )(info, *parts, w_k, w_v, q, o, lse)


def attend_last(distances, info, parts, w_k, w_v, q, o, lse, lats, w_o):
    return pl.pallas_call(
        functools.partial(attend_last_kernel, distances),
        out_shape=jax.ShapeDtypeStruct((FRAMES, 1, HALF, C2), BF16),
        in_specs=[SM] + [VM] * (len(parts) + 8),
        out_specs=pl.BlockSpec(memory_space=pl.ANY),
        scratch_shapes=attend_scratch(parts)
        + [
            pltpu.VMEM((FRAMES, HALF, C2), F32),
            pltpu.VMEM((FRAMES, HALF, C2), BF16),
            pltpu.SemaphoreType.DMA((4,)),
        ],
        compiler_params=pltpu.CompilerParams(vmem_limit_bytes=VMEM_ATTEND),
        cost_estimate=SMALL_COST,
        name="attend_last",
    )(info, *parts, w_k, w_v, q, o, lse, *lats, w_o)


def next_stretch(by):
    stretches, tiles = lax.axis_size("stretch"), lax.axis_size("tile")
    return [
        (s * tiles + t, (s + 1) * tiles + t + by)
        for s in range(stretches - 1)
        for t in range(tiles)
        if 0 <= t + by < tiles
    ]


def back_hops(count, ring):
    first = [(s, s + ring - 1 if s % ring == 0 else s - 1) for s in range(count - 2)]
    first = [(i, j) for i, j in first if j < count]
    return first, [(j, i + 2) for i, j in first]


def local(video, clip_table, w_spatial, w_temporal, w_down, w_query, w_key, w_value, w_out):
    position = lax.axis_index("stretch")
    ends = jnp.cumsum(clip_table[0])
    starts = ends - clip_table[0]
    member = (starts <= position) & (position < ends)
    offset = jnp.sum(jnp.where(member, position - starts, 0))
    is_last = member & (ends - 1 == position)
    valid = jnp.where(jnp.any(is_last), jnp.sum(jnp.where(is_last, clip_table[1], 0)), FRAMES)
    info = jnp.stack([offset, valid]).astype(jnp.int32)

    low, high, last, last_low, last_high = edges(video)
    up = send(low, "tile", 1)
    down = send(high, "tile", -1)
    before = send(last, "stretch", 1)
    before_up = lax.ppermute(last_low, ("stretch", "tile"), next_stretch(1))
    before_down = lax.ppermute(last_high, ("stretch", "tile"), next_stretch(-1))
    weights = front_weights(w_spatial, w_temporal, w_down)
    hop, hop_on = back_hops(lax.axis_size("stretch"), 4)

    lat_1, context = front(info, video, up, down, *weights)
    back = lax.ppermute(lat_1, "stretch", hop)
    lat_0 = front_first(info, video, before, before_up, before_down, context, *weights)
    one_0 = send(lat_0, "stretch", 1)
    lats = (lat_0, lat_1)
    q, o, lse = attend_own(lats, w_query, w_key, w_value)
    later, _ = lax.optimization_barrier((lat_1, lse))
    one_1 = send(later, "stretch", 1)
    two_0 = send(one_0, "stretch", 1)
    two_1 = lax.ppermute(back, "stretch", hop_on)
    o, lse = attend_more((1, 1), info, (one_0, one_1), w_key, w_value, q, o, lse)
    return attend_last((2, 2), info, (two_0, two_1), w_key, w_value, q, o, lse, lats, w_out)


def solution(mesh):
    in_specs = (P("stretch", "tile", None, None), P(), P(), P(), P(), P(), P(), P(), P())
    out_specs = P("stretch", "tile", None, None)
    return jax.shard_map(local, mesh=mesh, in_specs=in_specs, out_specs=out_specs, check_vma=False)
```

```python
import functools

import jax
import jax.numpy as jnp
from jax import lax
from jax.experimental import pallas as pl
from jax.experimental.pallas import tpu as pltpu
from jax.sharding import PartitionSpec as P

F32 = jnp.float32
BF16 = jnp.bfloat16
FRAMES = 17
COLS = 320
HALF = 160
C1 = 128
C2 = 256
BIG = 3.0e38
EDGE_STEP = 9
PARTS = (8, 9)
LARGE_COST = pl.CostEstimate(flops=3 * 10**10, bytes_accessed=10**7, transcendentals=0)
SMALL_COST = pl.CostEstimate(flops=10**6, bytes_accessed=10**4, transcendentals=0)
VM = pl.BlockSpec(memory_space=pltpu.VMEM)
SM = pl.BlockSpec(memory_space=pltpu.SMEM)
VMEM_EDGES = 60 * 2**20
VMEM_FRONT = 28 * 2**20
VMEM_ATTEND = 24 * 2**20


def shift_perm(axis, by):
    count = lax.axis_size(axis)
    return [(i, i + by) for i in range(count) if 0 <= i + by < count]


def send(x, axis, by):
    return lax.ppermute(x, axis, shift_perm(axis, by))


def spread_weights(w_conv, w_time, conv, time):
    zero = jnp.zeros((C1, C1), BF16)
    for b in range(3):
        for r in range(2):
            at = slice((2 * b + r) * C1, (2 * b + r + 1) * C1)
            for i in range(4):
                conv[i * C1 : (i + 1) * C1, at] = w_conv[i - r, b] if 0 <= i - r <= 2 else zero
    for i in range(3):
        for r in range(2):
            for c in range(2):
                block = w_time[i] * 0.5 if r == c else zero
                time[(2 * i + r) * C1 : (2 * i + r + 1) * C1, c * C1 : (c + 1) * C1] = block


def edge_kernel(video, low, high, last, last_low, last_high, sems):
    end = pl.ds(FRAMES - 2, 2)
    pairs = [
        (video.at[pl.ds(f, min(EDGE_STEP, FRAMES - f)), row], target.at[pl.ds(f, min(EDGE_STEP, FRAMES - f))])
        for row, target in ((1, low), (0, high))
        for f in range(0, FRAMES, EDGE_STEP)
    ]
    pairs += [
        (video.at[end], last),
        (video.at[end, 1], last_low),
        (video.at[end, 0], last_high),
    ]
    copies = [pltpu.make_async_copy(*pair, sems.at[i]) for i, pair in enumerate(pairs)]
    for copy in copies:
        copy.start()
    for copy in copies:
        copy.wait()


def edges(video):
    row = jax.ShapeDtypeStruct((FRAMES, COLS, C1), BF16)
    last_row = jax.ShapeDtypeStruct((2, COLS, C1), BF16)
    return pl.pallas_call(
        edge_kernel,
        out_shape=(row, row, jax.ShapeDtypeStruct((2, 2, COLS, C1), BF16), last_row, last_row),
        in_specs=[pl.BlockSpec(memory_space=pl.ANY)],
        out_specs=(VM,) * 5,
        scratch_shapes=[pltpu.SemaphoreType.DMA((3 + 2 * -(-FRAMES // EDGE_STEP),))],
        compiler_params=pltpu.CompilerParams(vmem_limit_bytes=VMEM_EDGES),
        cost_estimate=SMALL_COST,
        name="edges",
    )(video)


def weights_kernel(w_conv, w_time, w_down, conv, time, down):
    spread_weights(w_conv, w_time, conv, time)
    down[...] = w_down[...] * 0.5


def front_weights(w_conv, w_time, w_down):
    return pl.pallas_call(
        weights_kernel,
        out_shape=(
            jax.ShapeDtypeStruct((4 * C1, 6 * C1), BF16),
            jax.ShapeDtypeStruct((6 * C1, 2 * C1), BF16),
            jax.ShapeDtypeStruct((4 * C1, C2), BF16),
        ),
        in_specs=[VM] * 3,
        out_specs=(VM, VM, VM),
        compiler_params=pltpu.CompilerParams(vmem_limit_bytes=VMEM_FRONT),
        cost_estimate=SMALL_COST,
        name="front_weights",
    )(w_conv, w_time, w_down)


def conv_frames(first, at, count, vid, up, down, w_conv, planes):
    row = lax.broadcasted_iota(jnp.int32, (COLS, 2 * C1), 0)
    for f in range(count):
        g = first + f
        x = jnp.concatenate([up[g], vid[g, 0], vid[g, 1], down[g]], axis=1)
        y = jnp.dot(x, w_conv[...], preferred_element_type=F32)
        left = pltpu.roll(y[:, : 2 * C1], 1, 0)
        right = pltpu.roll(y[:, 4 * C1 :], COLS - 1, 0)
        plane = (
            y[:, 2 * C1 : 4 * C1]
            + jnp.where(row == 0, 0.0, left)
            + jnp.where(row == COLS - 1, 0.0, right)
        )
        planes[f + at] = plane.astype(BF16)


def latent_scratch(frames):
    return [pltpu.VMEM((4, 2 * COLS, C1), F32), pltpu.VMEM((frames * HALF, 4 * C1), BF16)]


def latent_frames(first, video, planes, mixed, bands, w_time, w_down, latent):
    frames = latent.shape[0]
    for g in range(frames):
        m_ref = mixed.at[g % 4]
        x = jnp.concatenate([planes[g], planes[g + 1], planes[g + 2]], axis=1)
        u = jnp.dot(x, w_time[...], preferred_element_type=F32)
        gate = u + u * jnp.tanh(u)
        residual = jnp.concatenate([video[first + g, 0], video[first + g, 1]], axis=1).astype(F32)
        m = residual + gate
        m_ref[0:COLS, :] = m[:, :C1]
        m_ref[COLS:, :] = m[:, C1:]
        p = m_ref[pl.ds(0, HALF, stride=2), :]
        q = m_ref[pl.ds(1, HALF, stride=2), :]
        r = m_ref[pl.ds(COLS, HALF, stride=2), :]
        s = m_ref[pl.ds(COLS + 1, HALF, stride=2), :]
        top, low = p + q, r + s
        top_d, low_d = p - q, r - s
        b = jnp.concatenate([top + low, top_d + low_d, top - low, top_d - low_d], axis=1)
        bands[g * HALF : (g + 1) * HALF] = b.astype(BF16)
    out = jnp.dot(bands[...], w_down[...], preferred_element_type=F32)
    latent[...] = out.astype(BF16).reshape(frames, HALF, C2)


def front_kernel(info, video, up, down, w_conv, w_time, w_down, latent, context, planes, mixed, bands):
    del info
    count = latent.shape[0]
    first = FRAMES - count
    conv_frames(0, 0, FRAMES, video, up, down, w_conv, planes)
    context[...] = planes[0:first]
    latent_frames(first, video, planes.at[pl.ds(first - 2, count + 2)], mixed, bands, w_time, w_down, latent)


def front(info, video, up, down, w_conv, w_time, w_down):
    first, count = PARTS
    return pl.pallas_call(
        front_kernel,
        out_shape=(
            jax.ShapeDtypeStruct((count, HALF, C2), BF16),
            jax.ShapeDtypeStruct((first, COLS, 2 * C1), BF16),
        ),
        in_specs=[SM] + [VM] * 6,
        out_specs=(VM,) * 2,
        scratch_shapes=[pltpu.VMEM((FRAMES, COLS, 2 * C1), BF16)] + latent_scratch(count),
        compiler_params=pltpu.CompilerParams(vmem_limit_bytes=VMEM_FRONT),
        cost_estimate=LARGE_COST,
        name="front",
    )(info, video, up, down, w_conv, w_time, w_down)


def front_first_kernel(info, video, before, before_up, before_down, context, w_conv, w_time, w_down,
                       latent, planes, mixed, bands):
    count = latent.shape[0]
    conv_frames(0, 0, 2, before, before_up, before_down, w_conv, planes)
    for f in range(2):
        planes[f] = jnp.where(info[0] == 0, context[0], planes[f])
    planes[2 : count + 2] = context[...]
    latent_frames(0, video, planes, mixed, bands, w_time, w_down, latent)


def front_first(info, video, before, before_up, before_down, context, w_conv, w_time, w_down):
    count = PARTS[0]
    return pl.pallas_call(
        front_first_kernel,
        out_shape=jax.ShapeDtypeStruct((count, HALF, C2), BF16),
        in_specs=[SM] + [VM] * 8,
        out_specs=VM,
        scratch_shapes=[pltpu.VMEM((count + 2, COLS, 2 * C1), BF16)] + latent_scratch(count),
        compiler_params=pltpu.CompilerParams(vmem_limit_bytes=VMEM_FRONT),
        cost_estimate=LARGE_COST,
        name="front_first",
    )(info, video, before, before_up, before_down, context, w_conv, w_time, w_down)


ROWS = FRAMES * 8
GROUPS = HALF // 8


def padded(frames):
    return -(-frames * 8 // 128) * 128


def normalize(x):
    return (x * lax.rsqrt(jnp.mean(x * x, axis=-1, keepdims=True) + 1e-6)).astype(BF16)


def project(parts, weights, targets):
    at = 0
    for part in parts:
        for f0 in range(0, part.shape[0], 6):
            frames = min(6, part.shape[0] - f0)
            x = normalize(part[f0 : f0 + frames].reshape(frames * HALF, C2).astype(F32))
            for w, scale, target in zip(weights, (1.0, 1.0, 1.0 / 16.0), targets):
                y = jnp.dot(x, w[...], preferred_element_type=F32)
                if scale != 1.0:
                    y = y * scale
                y = y.reshape(frames, GROUPS, 8, C2)
                for f in range(frames):
                    target[:, (at + f) * 8 : (at + f + 1) * 8, :] = y[f]
            at += frames


def attend_group(q, k, v, bound):
    pad = jnp.zeros((bound.shape[1] - k.shape[0], C2), BF16)
    k = jnp.concatenate([k.astype(BF16), pad], axis=0)
    v = jnp.concatenate([v.astype(BF16), pad], axis=0)
    scores = lax.dot_general(q.astype(BF16), k, (((1,), (1,)), ((), ())), preferred_element_type=F32)
    scores = jnp.minimum(scores, bound[...])
    top = jnp.max(scores, axis=-1, keepdims=True)
    e = jnp.exp(scores - top)
    total = jnp.sum(e, axis=-1, keepdims=True)
    return top, total, jnp.dot(e.astype(BF16), v, preferred_element_type=F32)


def positions(bound):
    r = lax.broadcasted_iota(jnp.int32, bound.shape, 0)
    c = lax.broadcasted_iota(jnp.int32, bound.shape, 1)
    same = jnp.bitwise_and(r, 7) == jnp.bitwise_and(c, 7)
    return same, jnp.right_shift(r, 3), jnp.right_shift(c, 3)


def attend_own_kernel(lat_0, lat_1, w_q, w_k, w_v, q_out, o_out, lse_out, ks, vs, bound):
    same, t, s = positions(bound)
    bound[...] = jnp.where(same & (s <= t), BIG, -1e30)
    project((lat_0, lat_1), (w_k, w_v, w_q), (ks, vs, q_out))

    def group(g, _):
        top, total, o = attend_group(q_out[g], ks[g], vs[g], bound)
        o_out[g] = o / total
        lse_out[g] = jnp.broadcast_to(top + jnp.log(total), (ROWS, 128))
        return 0

    lax.fori_loop(0, GROUPS, group, 0, unroll=10)


def merge(top, total, o, o_before, lse_before):
    top = jnp.broadcast_to(top, lse_before.shape)
    total = jnp.broadcast_to(total, lse_before.shape)
    most = jnp.maximum(lse_before, top)
    old, new = jnp.exp(lse_before - most), jnp.exp(top - most)
    whole = old + total * new
    share = 1.0 / whole
    old, new = old * share, new * share
    o = o_before * jnp.concatenate([old, old], axis=1) + o * jnp.concatenate([new, new], axis=1)
    return o, most + jnp.log(whole)


def part_bound(info, parts, distances, bound):
    same, _, s = positions(bound)
    offset = info[0]
    allowed = jnp.zeros(bound.shape, jnp.bool_)
    at = 0
    for part, distance in zip(parts, distances):
        end = at + part.shape[0]
        first = jnp.where(offset >= distance, at, end)
        allowed = allowed | ((s >= first) & (s < end))
        at = end
    bound[...] = jnp.where(same & allowed, BIG, -1e30)


def attend_more_kernel(distances, info, *refs):
    parts, refs = refs[: len(distances)], refs[len(distances) :]
    w_k, w_v, q_in, o_in, lse_in, o_out, lse_out, ks, vs, bound = refs
    part_bound(info, parts, distances, bound)
    project(parts, (w_k, w_v), (ks, vs))

    def group(g, _):
        top, total, o = attend_group(q_in[g], ks[g], vs[g], bound)
        o, lse = merge(top, total, o, o_in[g], lse_in[g])
        o_out[g] = o
        lse_out[g] = lse
        return 0

    lax.fori_loop(0, GROUPS, group, 0, unroll=10)


def attend_last_kernel(distances, info, *refs):
    parts, refs = refs[: len(distances)], refs[len(distances) :]
    w_k, w_v, q_in, o_in, lse_in, lat_0, lat_1, w_o, out, ks, vs, bound, attended, staged, sems = refs
    part_bound(info, parts, distances, bound)
    project(parts, (w_k, w_v), (ks, vs))

    def group(g, _):
        top, total, o = attend_group(q_in[g], ks[g], vs[g], bound)
        o, _ = merge(top, total, o, o_in[g], lse_in[g])
        attended[:, pl.ds(pl.multiple_of(g * 8, 8), 8), :] = o.reshape(FRAMES, 8, C2)
        return 0

    lax.fori_loop(0, GROUPS, group, 0, unroll=10)
    valid = info[1]
    at = 0
    copies = []
    for part in (lat_0, lat_1):
        for f0 in range(0, part.shape[0], 6):
            frames = min(6, part.shape[0] - f0)
            a = attended[at : at + frames].reshape(frames * HALF, C2).astype(BF16)
            update = jnp.dot(a, w_o[...], preferred_element_type=F32).reshape(frames, HALF, C2)
            for f in range(frames):
                value = part[f0 + f].astype(F32) + update[f]
                staged[at + f] = jnp.where(at + f < valid, value, 0.0).astype(BF16)
            done = pl.ds(at, frames)
            copies.append(pltpu.make_async_copy(staged.at[done], out.at[done, 0], sems.at[len(copies)]))
            copies[-1].start()
            at += frames
    for copy in copies:
        copy.wait()


BY_GROUP = jax.ShapeDtypeStruct((GROUPS, ROWS, C2), F32)
BY_GROUP_LSE = jax.ShapeDtypeStruct((GROUPS, ROWS, 128), F32)


def attend_scratch(parts):
    frames = sum(part.shape[0] for part in parts)
    return [
        pltpu.VMEM((GROUPS, frames * 8, C2), F32),
        pltpu.VMEM((GROUPS, frames * 8, C2), F32),
        pltpu.VMEM((ROWS, padded(frames)), F32),
    ]


def attend_own(lats, w_q, w_k, w_v):
    return pl.pallas_call(
        attend_own_kernel,
        out_shape=(BY_GROUP, BY_GROUP, BY_GROUP_LSE),
        in_specs=[VM] * 5,
        out_specs=(VM, VM, VM),
        scratch_shapes=attend_scratch(lats),
        compiler_params=pltpu.CompilerParams(vmem_limit_bytes=VMEM_ATTEND),
        cost_estimate=LARGE_COST,
        name="attend_own",
    )(*lats, w_q, w_k, w_v)


def attend_more(distances, info, parts, w_k, w_v, q, o, lse):
    return pl.pallas_call(
        functools.partial(attend_more_kernel, distances),
        out_shape=(BY_GROUP, BY_GROUP_LSE),
        in_specs=[SM] + [VM] * (len(parts) + 5),
        out_specs=(VM, VM),
        scratch_shapes=attend_scratch(parts),
        compiler_params=pltpu.CompilerParams(vmem_limit_bytes=VMEM_ATTEND),
        cost_estimate=SMALL_COST,
        name="attend_more",
    )(info, *parts, w_k, w_v, q, o, lse)


def attend_last(distances, info, parts, w_k, w_v, q, o, lse, lats, w_o):
    return pl.pallas_call(
        functools.partial(attend_last_kernel, distances),
        out_shape=jax.ShapeDtypeStruct((FRAMES, 1, HALF, C2), BF16),
        in_specs=[SM] + [VM] * (len(parts) + 8),
        out_specs=pl.BlockSpec(memory_space=pl.ANY),
        scratch_shapes=attend_scratch(parts)
        + [
            pltpu.VMEM((FRAMES, HALF, C2), F32),
            pltpu.VMEM((FRAMES, HALF, C2), BF16),
            pltpu.SemaphoreType.DMA((4,)),
        ],
        compiler_params=pltpu.CompilerParams(vmem_limit_bytes=VMEM_ATTEND),
        cost_estimate=SMALL_COST,
        name="attend_last",
    )(info, *parts, w_k, w_v, q, o, lse, *lats, w_o)


def next_stretch(by):
    stretches, tiles = lax.axis_size("stretch"), lax.axis_size("tile")
    return [
        (s * tiles + t, (s + 1) * tiles + t + by)
        for s in range(stretches - 1)
        for t in range(tiles)
        if 0 <= t + by < tiles
    ]


def back_hops(count, ring):
    first = [(s, s + ring - 1 if s % ring == 0 else s - 1) for s in range(count - 2)]
    first = [(i, j) for i, j in first if j < count]
    return first, [(j, i + 2) for i, j in first]


def local(video, clip_table, w_spatial, w_temporal, w_down, w_query, w_key, w_value, w_out):
    position = lax.axis_index("stretch")
    ends = jnp.cumsum(clip_table[0])
    starts = ends - clip_table[0]
    member = (starts <= position) & (position < ends)
    offset = jnp.sum(jnp.where(member, position - starts, 0))
    is_last = member & (ends - 1 == position)
    valid = jnp.where(jnp.any(is_last), jnp.sum(jnp.where(is_last, clip_table[1], 0)), FRAMES)
    info = jnp.stack([offset, valid]).astype(jnp.int32)

    low, high, last, last_low, last_high = edges(video)
    up = send(low, "tile", 1)
    down = send(high, "tile", -1)
    before = send(last, "stretch", 1)
    before_up = lax.ppermute(last_low, ("stretch", "tile"), next_stretch(1))
    before_down = lax.ppermute(last_high, ("stretch", "tile"), next_stretch(-1))
    weights = front_weights(w_spatial, w_temporal, w_down)
    hop, hop_on = back_hops(lax.axis_size("stretch"), 4)

    lat_1, context = front(info, video, up, down, *weights)
    back = lax.ppermute(lat_1, "stretch", hop)
    lat_0 = front_first(info, video, before, before_up, before_down, context, *weights)
    one_0 = send(lat_0, "stretch", 1)
    lats = (lat_0, lat_1)
    q, o, lse = attend_own(lats, w_query, w_key, w_value)
    later, _ = lax.optimization_barrier((lat_1, lse))
    one_1 = send(later, "stretch", 1)
    two_0 = send(one_0, "stretch", 1)
    two_1 = lax.ppermute(back, "stretch", hop_on)
    o, lse = attend_more((1, 1), info, (one_0, one_1), w_key, w_value, q, o, lse)
    return attend_last((2, 2), info, (two_0, two_1), w_key, w_value, q, o, lse, lats, w_out)


def solution(mesh):
    in_specs = (P("stretch", "tile", None, None), P(), P(), P(), P(), P(), P(), P(), P())
    out_specs = P("stretch", "tile", None, None)
    return jax.shard_map(local, mesh=mesh, in_specs=in_specs, out_specs=out_specs, check_vma=False)
```

```python
import functools

import jax
import jax.numpy as jnp
from jax import lax
from jax.experimental import pallas as pl
from jax.experimental.pallas import tpu as pltpu
from jax.sharding import PartitionSpec as P

F32 = jnp.float32
BF16 = jnp.bfloat16
FRAMES = 17
COLS = 320
HALF = 160
C1 = 128
C2 = 256
BIG = 3.0e38
EDGE_STEP = 9
PARTS = (8, 9)
LARGE_COST = pl.CostEstimate(flops=3 * 10**10, bytes_accessed=10**7, transcendentals=0)
SMALL_COST = pl.CostEstimate(flops=10**6, bytes_accessed=10**4, transcendentals=0)
VM = pl.BlockSpec(memory_space=pltpu.VMEM)
SM = pl.BlockSpec(memory_space=pltpu.SMEM)
VMEM_EDGES = 60 * 2**20
VMEM_FRONT = 28 * 2**20
VMEM_ATTEND = 24 * 2**20


def shift_perm(axis, by):
    count = lax.axis_size(axis)
    return [(i, i + by) for i in range(count) if 0 <= i + by < count]


def send(x, axis, by):
    return lax.ppermute(x, axis, shift_perm(axis, by))


def spread_weights(w_conv, w_time, conv, time):
    zero = jnp.zeros((C1, C1), BF16)
    for b in range(3):
        for r in range(2):
            at = slice((2 * b + r) * C1, (2 * b + r + 1) * C1)
            for i in range(4):
                conv[i * C1 : (i + 1) * C1, at] = w_conv[i - r, b] if 0 <= i - r <= 2 else zero
    for i in range(3):
        for r in range(2):
            for c in range(2):
                block = w_time[i] * 0.5 if r == c else zero
                time[(2 * i + r) * C1 : (2 * i + r + 1) * C1, c * C1 : (c + 1) * C1] = block


def edge_kernel(video, low, high, last, last_low, last_high, sems):
    end = pl.ds(FRAMES - 2, 2)
    pairs = [
        (video.at[pl.ds(f, min(EDGE_STEP, FRAMES - f)), row], target.at[pl.ds(f, min(EDGE_STEP, FRAMES - f))])
        for row, target in ((1, low), (0, high))
        for f in range(0, FRAMES, EDGE_STEP)
    ]
    pairs += [
        (video.at[end], last),
        (video.at[end, 1], last_low),
        (video.at[end, 0], last_high),
    ]
    copies = [pltpu.make_async_copy(*pair, sems.at[i]) for i, pair in enumerate(pairs)]
    for copy in copies:
        copy.start()
    for copy in copies:
        copy.wait()


def edges(video):
    row = jax.ShapeDtypeStruct((FRAMES, COLS, C1), BF16)
    last_row = jax.ShapeDtypeStruct((2, COLS, C1), BF16)
    return pl.pallas_call(
        edge_kernel,
        out_shape=(row, row, jax.ShapeDtypeStruct((2, 2, COLS, C1), BF16), last_row, last_row),
        in_specs=[pl.BlockSpec(memory_space=pl.ANY)],
        out_specs=(VM,) * 5,
        scratch_shapes=[pltpu.SemaphoreType.DMA((3 + 2 * -(-FRAMES // EDGE_STEP),))],
        compiler_params=pltpu.CompilerParams(vmem_limit_bytes=VMEM_EDGES),
        cost_estimate=SMALL_COST,
        name="edges",
    )(video)


def weights_kernel(w_conv, w_time, w_down, conv, time, down):
    spread_weights(w_conv, w_time, conv, time)
    down[...] = w_down[...] * 0.5


def front_weights(w_conv, w_time, w_down):
    return pl.pallas_call(
        weights_kernel,
        out_shape=(
            jax.ShapeDtypeStruct((4 * C1, 6 * C1), BF16),
            jax.ShapeDtypeStruct((6 * C1, 2 * C1), BF16),
            jax.ShapeDtypeStruct((4 * C1, C2), BF16),
        ),
        in_specs=[VM] * 3,
        out_specs=(VM, VM, VM),
        compiler_params=pltpu.CompilerParams(vmem_limit_bytes=VMEM_FRONT),
        cost_estimate=SMALL_COST,
        name="front_weights",
    )(w_conv, w_time, w_down)


def conv_frames(first, at, count, vid, up, down, w_conv, planes):
    row = lax.broadcasted_iota(jnp.int32, (COLS, 2 * C1), 0)
    for f in range(count):
        g = first + f
        x = jnp.concatenate([up[g], vid[g, 0], vid[g, 1], down[g]], axis=1)
        y = jnp.dot(x, w_conv[...], preferred_element_type=F32)
        left = pltpu.roll(y[:, : 2 * C1], 1, 0)
        right = pltpu.roll(y[:, 4 * C1 :], COLS - 1, 0)
        plane = (
            y[:, 2 * C1 : 4 * C1]
            + jnp.where(row == 0, 0.0, left)
            + jnp.where(row == COLS - 1, 0.0, right)
        )
        planes[f + at] = plane.astype(BF16)


def latent_scratch(frames):
    return [pltpu.VMEM((4, 2 * COLS, C1), F32), pltpu.VMEM((frames * HALF, 4 * C1), BF16)]


def latent_frames(first, video, planes, mixed, bands, w_time, w_down, latent):
    frames = latent.shape[0]
    for g in range(frames):
        m_ref = mixed.at[g % 4]
        x = jnp.concatenate([planes[g], planes[g + 1], planes[g + 2]], axis=1)
        u = jnp.dot(x, w_time[...], preferred_element_type=F32)
        gate = u + u * jnp.tanh(u)
        residual = jnp.concatenate([video[first + g, 0], video[first + g, 1]], axis=1).astype(F32)
        m = residual + gate
        m_ref[0:COLS, :] = m[:, :C1]
        m_ref[COLS:, :] = m[:, C1:]
        p = m_ref[pl.ds(0, HALF, stride=2), :]
        q = m_ref[pl.ds(1, HALF, stride=2), :]
        r = m_ref[pl.ds(COLS, HALF, stride=2), :]
        s = m_ref[pl.ds(COLS + 1, HALF, stride=2), :]
        top, low = p + q, r + s
        top_d, low_d = p - q, r - s
        b = jnp.concatenate([top + low, top_d + low_d, top - low, top_d - low_d], axis=1)
        bands[g * HALF : (g + 1) * HALF] = b.astype(BF16)
    out = jnp.dot(bands[...], w_down[...], preferred_element_type=F32)
    latent[...] = out.astype(BF16).reshape(frames, HALF, C2)


def front_kernel(info, video, up, down, w_conv, w_time, w_down, latent, context, planes, mixed, bands):
    del info
    count = latent.shape[0]
    first = FRAMES - count
    conv_frames(0, 0, FRAMES, video, up, down, w_conv, planes)
    context[...] = planes[0:first]
    latent_frames(first, video, planes.at[pl.ds(first - 2, count + 2)], mixed, bands, w_time, w_down, latent)


def front(info, video, up, down, w_conv, w_time, w_down):
    first, count = PARTS
    return pl.pallas_call(
        front_kernel,
        out_shape=(
            jax.ShapeDtypeStruct((count, HALF, C2), BF16),
            jax.ShapeDtypeStruct((first, COLS, 2 * C1), BF16),
        ),
        in_specs=[SM] + [VM] * 6,
        out_specs=(VM,) * 2,
        scratch_shapes=[pltpu.VMEM((FRAMES, COLS, 2 * C1), BF16)] + latent_scratch(count),
        compiler_params=pltpu.CompilerParams(vmem_limit_bytes=VMEM_FRONT),
        cost_estimate=LARGE_COST,
        name="front",
    )(info, video, up, down, w_conv, w_time, w_down)


def front_first_kernel(info, video, before, before_up, before_down, context, w_conv, w_time, w_down,
                       latent, planes, mixed, bands):
    count = latent.shape[0]
    conv_frames(0, 0, 2, before, before_up, before_down, w_conv, planes)
    for f in range(2):
        planes[f] = jnp.where(info[0] == 0, context[0], planes[f])
    planes[2 : count + 2] = context[...]
    latent_frames(0, video, planes, mixed, bands, w_time, w_down, latent)


def front_first(info, video, before, before_up, before_down, context, w_conv, w_time, w_down):
    count = PARTS[0]
    return pl.pallas_call(
        front_first_kernel,
        out_shape=jax.ShapeDtypeStruct((count, HALF, C2), BF16),
        in_specs=[SM] + [VM] * 8,
        out_specs=VM,
        scratch_shapes=[pltpu.VMEM((count + 2, COLS, 2 * C1), BF16)] + latent_scratch(count),
        compiler_params=pltpu.CompilerParams(vmem_limit_bytes=VMEM_FRONT),
        cost_estimate=LARGE_COST,
        name="front_first",
    )(info, video, before, before_up, before_down, context, w_conv, w_time, w_down)


ROWS = FRAMES * 8
GROUPS = HALF // 8


def padded(frames):
    return -(-frames * 8 // 128) * 128


def normalize(x):
    return (x * lax.rsqrt(jnp.mean(x * x, axis=-1, keepdims=True) + 1e-6)).astype(BF16)


def project(parts, weights, targets):
    at = 0
    for part in parts:
        for f0 in range(0, part.shape[0], 6):
            frames = min(6, part.shape[0] - f0)
            x = normalize(part[f0 : f0 + frames].reshape(frames * HALF, C2).astype(F32))
            for w, scale, target in zip(weights, (1.0, 1.0, 1.0 / 16.0), targets):
                y = jnp.dot(x, w[...], preferred_element_type=F32)
                if scale != 1.0:
                    y = y * scale
                y = y.reshape(frames, GROUPS, 8, C2)
                for f in range(frames):
                    target[:, (at + f) * 8 : (at + f + 1) * 8, :] = y[f]
            at += frames


def attend_group(q, k, v, bound):
    pad = jnp.zeros((bound.shape[1] - k.shape[0], C2), BF16)
    k = jnp.concatenate([k.astype(BF16), pad], axis=0)
    v = jnp.concatenate([v.astype(BF16), pad], axis=0)
    scores = lax.dot_general(q.astype(BF16), k, (((1,), (1,)), ((), ())), preferred_element_type=F32)
    scores = jnp.minimum(scores, bound[...])
    top = jnp.max(scores, axis=-1, keepdims=True)
    e = jnp.exp(scores - top)
    total = jnp.sum(e, axis=-1, keepdims=True)
    return top, total, jnp.dot(e.astype(BF16), v, preferred_element_type=F32)


def positions(bound):
    r = lax.broadcasted_iota(jnp.int32, bound.shape, 0)
    c = lax.broadcasted_iota(jnp.int32, bound.shape, 1)
    same = jnp.bitwise_and(r, 7) == jnp.bitwise_and(c, 7)
    return same, jnp.right_shift(r, 3), jnp.right_shift(c, 3)


def attend_own_kernel(lat_0, lat_1, w_q, w_k, w_v, q_out, o_out, lse_out, ks, vs, bound):
    same, t, s = positions(bound)
    bound[...] = jnp.where(same & (s <= t), BIG, -1e30)
    project((lat_0, lat_1), (w_k, w_v, w_q), (ks, vs, q_out))

    def group(g, _):
        top, total, o = attend_group(q_out[g], ks[g], vs[g], bound)
        o_out[g] = o / total
        lse_out[g] = jnp.broadcast_to(top + jnp.log(total), (ROWS, 128))
        return 0

    lax.fori_loop(0, GROUPS, group, 0, unroll=20)


def merge(top, total, o, o_before, lse_before):
    top = jnp.broadcast_to(top, lse_before.shape)
    total = jnp.broadcast_to(total, lse_before.shape)
    most = jnp.maximum(lse_before, top)
    old, new = jnp.exp(lse_before - most), jnp.exp(top - most)
    whole = old + total * new
    share = 1.0 / whole
    old, new = old * share, new * share
    o = o_before * jnp.concatenate([old, old], axis=1) + o * jnp.concatenate([new, new], axis=1)
    return o, most + jnp.log(whole)


def part_bound(info, parts, distances, bound):
    same, _, s = positions(bound)
    offset = info[0]
    allowed = jnp.zeros(bound.shape, jnp.bool_)
    at = 0
    for part, distance in zip(parts, distances):
        end = at + part.shape[0]
        first = jnp.where(offset >= distance, at, end)
        allowed = allowed | ((s >= first) & (s < end))
        at = end
    bound[...] = jnp.where(same & allowed, BIG, -1e30)


def attend_more_kernel(distances, info, *refs):
    parts, refs = refs[: len(distances)], refs[len(distances) :]
    w_k, w_v, q_in, o_in, lse_in, o_out, lse_out, ks, vs, bound = refs
    part_bound(info, parts, distances, bound)
    project(parts, (w_k, w_v), (ks, vs))

    def group(g, _):
        top, total, o = attend_group(q_in[g], ks[g], vs[g], bound)
        o, lse = merge(top, total, o, o_in[g], lse_in[g])
        o_out[g] = o
        lse_out[g] = lse
        return 0

    lax.fori_loop(0, GROUPS, group, 0, unroll=20)


def attend_last_kernel(distances, info, *refs):
    parts, refs = refs[: len(distances)], refs[len(distances) :]
    w_k, w_v, q_in, o_in, lse_in, lat_0, lat_1, w_o, out, ks, vs, bound, attended, staged, sems = refs
    part_bound(info, parts, distances, bound)
    project(parts, (w_k, w_v), (ks, vs))

    def group(g, _):
        top, total, o = attend_group(q_in[g], ks[g], vs[g], bound)
        o, _ = merge(top, total, o, o_in[g], lse_in[g])
        attended[:, pl.ds(pl.multiple_of(g * 8, 8), 8), :] = o.reshape(FRAMES, 8, C2)
        return 0

    lax.fori_loop(0, GROUPS, group, 0, unroll=20)
    valid = info[1]
    at = 0
    copies = []
    for part in (lat_0, lat_1):
        for f0 in range(0, part.shape[0], 6):
            frames = min(6, part.shape[0] - f0)
            a = attended[at : at + frames].reshape(frames * HALF, C2).astype(BF16)
            update = jnp.dot(a, w_o[...], preferred_element_type=F32).reshape(frames, HALF, C2)
            for f in range(frames):
                value = part[f0 + f].astype(F32) + update[f]
                staged[at + f] = jnp.where(at + f < valid, value, 0.0).astype(BF16)
            done = pl.ds(at, frames)
            copies.append(pltpu.make_async_copy(staged.at[done], out.at[done, 0], sems.at[len(copies)]))
            copies[-1].start()
            at += frames
    for copy in copies:
        copy.wait()


BY_GROUP = jax.ShapeDtypeStruct((GROUPS, ROWS, C2), F32)
BY_GROUP_LSE = jax.ShapeDtypeStruct((GROUPS, ROWS, 128), F32)


def attend_scratch(parts):
    frames = sum(part.shape[0] for part in parts)
    return [
        pltpu.VMEM((GROUPS, frames * 8, C2), F32),
        pltpu.VMEM((GROUPS, frames * 8, C2), F32),
        pltpu.VMEM((ROWS, padded(frames)), F32),
    ]


def attend_own(lats, w_q, w_k, w_v):
    return pl.pallas_call(
        attend_own_kernel,
        out_shape=(BY_GROUP, BY_GROUP, BY_GROUP_LSE),
        in_specs=[VM] * 5,
        out_specs=(VM, VM, VM),
        scratch_shapes=attend_scratch(lats),
        compiler_params=pltpu.CompilerParams(vmem_limit_bytes=VMEM_ATTEND),
        cost_estimate=LARGE_COST,
        name="attend_own",
    )(*lats, w_q, w_k, w_v)


def attend_more(distances, info, parts, w_k, w_v, q, o, lse):
    return pl.pallas_call(
        functools.partial(attend_more_kernel, distances),
        out_shape=(BY_GROUP, BY_GROUP_LSE),
        in_specs=[SM] + [VM] * (len(parts) + 5),
        out_specs=(VM, VM),
        scratch_shapes=attend_scratch(parts),
        compiler_params=pltpu.CompilerParams(vmem_limit_bytes=VMEM_ATTEND),
        cost_estimate=SMALL_COST,
        name="attend_more",
    )(info, *parts, w_k, w_v, q, o, lse)


def attend_last(distances, info, parts, w_k, w_v, q, o, lse, lats, w_o):
    return pl.pallas_call(
        functools.partial(attend_last_kernel, distances),
        out_shape=jax.ShapeDtypeStruct((FRAMES, 1, HALF, C2), BF16),
        in_specs=[SM] + [VM] * (len(parts) + 8),
        out_specs=pl.BlockSpec(memory_space=pl.ANY),
        scratch_shapes=attend_scratch(parts)
        + [
            pltpu.VMEM((FRAMES, HALF, C2), F32),
            pltpu.VMEM((FRAMES, HALF, C2), BF16),
            pltpu.SemaphoreType.DMA((4,)),
        ],
        compiler_params=pltpu.CompilerParams(vmem_limit_bytes=VMEM_ATTEND),
        cost_estimate=SMALL_COST,
        name="attend_last",
    )(info, *parts, w_k, w_v, q, o, lse, *lats, w_o)


def next_stretch(by):
    stretches, tiles = lax.axis_size("stretch"), lax.axis_size("tile")
    return [
        (s * tiles + t, (s + 1) * tiles + t + by)
        for s in range(stretches - 1)
        for t in range(tiles)
        if 0 <= t + by < tiles
    ]


def back_hops(count, ring):
    first = [(s, s + ring - 1 if s % ring == 0 else s - 1) for s in range(count - 2)]
    first = [(i, j) for i, j in first if j < count]
    return first, [(j, i + 2) for i, j in first]


def local(video, clip_table, w_spatial, w_temporal, w_down, w_query, w_key, w_value, w_out):
    position = lax.axis_index("stretch")
    ends = jnp.cumsum(clip_table[0])
    starts = ends - clip_table[0]
    member = (starts <= position) & (position < ends)
    offset = jnp.sum(jnp.where(member, position - starts, 0))
    is_last = member & (ends - 1 == position)
    valid = jnp.where(jnp.any(is_last), jnp.sum(jnp.where(is_last, clip_table[1], 0)), FRAMES)
    info = jnp.stack([offset, valid]).astype(jnp.int32)

    low, high, last, last_low, last_high = edges(video)
    up = send(low, "tile", 1)
    down = send(high, "tile", -1)
    before = send(last, "stretch", 1)
    before_up = lax.ppermute(last_low, ("stretch", "tile"), next_stretch(1))
    before_down = lax.ppermute(last_high, ("stretch", "tile"), next_stretch(-1))
    weights = front_weights(w_spatial, w_temporal, w_down)
    hop, hop_on = back_hops(lax.axis_size("stretch"), 4)

    lat_1, context = front(info, video, up, down, *weights)
    back = lax.ppermute(lat_1, "stretch", hop)
    lat_0 = front_first(info, video, before, before_up, before_down, context, *weights)
    one_0 = send(lat_0, "stretch", 1)
    lats = (lat_0, lat_1)
    q, o, lse = attend_own(lats, w_query, w_key, w_value)
    later, _ = lax.optimization_barrier((lat_1, lse))
    one_1 = send(later, "stretch", 1)
    two_0 = send(one_0, "stretch", 1)
    two_1 = lax.ppermute(back, "stretch", hop_on)
    o, lse = attend_more((1, 1), info, (one_0, one_1), w_key, w_value, q, o, lse)
    return attend_last((2, 2), info, (two_0, two_1), w_key, w_value, q, o, lse, lats, w_out)


def solution(mesh):
    in_specs = (P("stretch", "tile", None, None), P(), P(), P(), P(), P(), P(), P(), P())
    out_specs = P("stretch", "tile", None, None)
    return jax.shard_map(local, mesh=mesh, in_specs=in_specs, out_specs=out_specs, check_vma=False)
```
